32 devices in a mesh: groups: 2 (over y), sub: 4 (over z), beam: 4 (over x, core).
Axes of the slice: x: 2, y: 2, z: 4, core: 2. Of those that a mesh axis runs over, the one named last changes fastest.
Arguments:
- pulses: float32 [16384, 2, 384], P(('groups', 'sub', 'beam')), parts along dimension 0, may hold values from -6 to 6
- owners: int32 [16384, 1], P(('groups', 'sub', 'beam')), parts along dimension 0, may hold values from 0 to 3; in each aligned block of 512 rows (0 to 511, 512 to 1023, ...) at most 256 rows name the same one
- interp: bfloat16 [2, 2, 4, 2, 128, 128], P(None, None, 'beam'), may hold values from -0.375 to 0.375
- pattern: int32 [2, 4, 2], replicated, may hold values from 0 to 3
Outputs:
- image: bfloat16 [8, 512, 2, 384], P(('groups', 'sub'), 'beam'), parts along dimension 0
The draws below stay inside these ranges and needn't reach their ends.
There are 2 independent parts, one for each index of `groups`. The reference program is written for one: setup_inputs(seed, part) draws one part's arguments, and reference() takes and returns one part's arrays. A program takes and returns all parts, laid end to end along the dimension named above; an argument that names none is the same for every part. Nothing has to cross between parts.
Inputs may be any that keep to these rules, and one draw needn't show every extreme that they name: `owners`: at most 256 of the pulses held by one device name the same owner.
All inputs are finite; a program needn't handle non-finite values.
Results may differ from the reference program's by a relative error of at most 0.0057.
Values may be sent and summed in bfloat16 or wider, within the bound.
A program may use at most 64 MiB of HBM per device.

```python
import math
import jax
import jax.numpy as jnp
import numpy as np
from jax import lax

P_DEV = 512
RANGE = 384
TILE = 128
TAPS = 2
LEVELS = 2
CAP = 256
PULSES = 8192
TILES = 4
BEAMS = 512
N_SUB = 4
N_BEAM = 4


def with_ends(result, rng, least, top_value):
    shape = result.shape
    spot = [jax.random.randint(jax.random.fold_in(rng, axis), (), 0, shape[axis]) for axis in range(len(shape))]
    result = result.at[tuple(spot)].set(least)
    longest = shape.index(max(shape))
    spot[longest] = (spot[longest] + 1) % shape[longest]
    return result.at[tuple(spot)].set(top_value)


def levels(stream_key, dims, pieces, low, largest):
    level, own = 1.0, jax.random.fold_in(stream_key, 6)
    for axis_at, parts in pieces:
        heights = jnp.exp(jax.random.uniform(jax.random.fold_in(own, axis_at), (parts,), jnp.float32, low / len(pieces), largest / len(pieces)))
        level = level * jnp.repeat(heights, dims[axis_at] // parts).reshape([-1 if axis == axis_at else 1 for axis in range(len(dims))])
    return level


def deal_out(stream_key, own, number, rows, count, top, reach, slope):
    ranking = jax.random.permutation(stream_key, count)
    heavy_load, common = shares(count, rows * top, reach, slope, True), shares(count, rows * top, reach, slope, False)
    places = jnp.arange(count)

    def named(lengths, turn):
        used = int((lengths > 0).sum())
        fixed = max(1, used // 4)
        moved = fixed + (places - fixed + turn * (used - fixed)) % max(1, count - fixed)
        return jnp.zeros((count,), jnp.int32).at[ranking[jnp.where(places < fixed, places, moved)]].set(jnp.asarray(lengths, jnp.int32))

    lengths = jnp.where(number % 4 == 0, named(heavy_load, number // 4), named(common, number - number // 4 - 1))
    mixed = jax.random.permutation(jax.random.fold_in(own, 3), count)
    giver, receiver = mixed[0:count // 2 * 2:2], mixed[1:count // 2 * 2:2]
    margin = jnp.minimum(lengths[giver] - 1, reach - lengths[receiver]) // 2
    margin = jnp.where((giver == ranking[0]) | (receiver == ranking[0]) | (lengths[receiver] == 0), 0, jnp.maximum(margin, 0))
    moved = jax.random.randint(jax.random.fold_in(own, 4), (count // 2,), 0, 1 << 20) % (margin + 1)
    lengths = lengths.at[giver].add(-moved).at[receiver].add(moved)
    members = jnp.searchsorted(jnp.cumsum(lengths), jnp.arange(rows * top), side="right").astype(jnp.int32)
    grid = members.reshape(top, rows).T
    grid = grid[jax.random.permutation(jax.random.fold_in(own, 1), rows)]
    turn = jax.random.randint(jax.random.fold_in(own, 2), (rows, 1), 0, top)
    return jnp.take_along_axis(grid, (jnp.arange(top)[None, :] + turn) % top, axis=1)


def shares(count, total, reach, lean, full):
    weights = [(1 << 20) // math.isqrt(rank ** lean) + 1 for rank in range(1, count + 1)]
    largest = reach if full else min(reach, max(-(-total // count), total * weights[0] // sum(weights)))
    least = 1 if total - largest >= count - 1 else 0
    given, rest = [largest] + [least] * (count - 1), total - largest - least * (count - 1)
    while rest > 0:
        candidates = [i for i in range(1, count) if given[i] < largest] or [i for i in range(1, count) if given[i] < reach]
        mass, left = sum([weights[i] for i in candidates]), rest
        for i in candidates:
            more = min(reach - given[i], max(1, left * weights[i] // mass), rest)
            given[i] = given[i] + more
            rest = rest - more
    return np.array(given)


def normal_values(own_key, dims, width, limit, shards=(), held_as=jnp.bfloat16):
    drawn = width * jax.random.normal(own_key, dims, jnp.float32)
    if shards:
        drawn = drawn * levels(own_key, dims, shards, -0.22, 0.18)
    return jnp.clip(drawn, -limit, limit).astype(held_as)


def setup_inputs(seed: int = 0, part: int = 0) -> dict:
    keys = jax.random.split(jax.random.key(seed), 5)
    part_splits = jax.random.split(jax.random.fold_in(keys[4], part), 5)
    pulses = normal_values(part_splits[0], (PULSES, 2, RANGE), 1.0, 6.0, ((0, 16),), jnp.float32)
    owners_keys = jax.random.split(jax.random.fold_in(part_splits[1], 1), PULSES // P_DEV)
    owners_turns = jax.random.permutation(jax.random.fold_in(part_splits[1], 3), PULSES // P_DEV)
    owners = jax.vmap(lambda own, number: deal_out(jax.random.fold_in(part_splits[1], 2), own, number, P_DEV, N_SUB, 1, CAP, 2))(owners_keys, owners_turns).reshape((PULSES, 1))
    interp = normal_values(keys[2], (LEVELS, 2, TILES, TAPS, TILE, TILE), (TAPS * TILE) ** -0.5, 0.375, ((2, 4),))
    pattern = with_ends(jax.random.randint(keys[3], (LEVELS, TILES, TAPS), 0, TILES), jax.random.fold_in(keys[3], 1), 0, TILES - 1).astype(jnp.int32)
    return {"pulses": pulses, "owners": owners, "interp": interp, "pattern": pattern}


two_pi = 2.0 * math.pi
phase_modulus = 1021

def steer_terms(beam_rows, sample_positions, beam_count):
    turns = beam_rows[:, None] * sample_positions[None, :] % beam_count
    angle = turns.astype(jnp.float32) * (two_pi / beam_count)
    return (jnp.cos(angle), jnp.sin(angle))

def beamform(cosine, sine, samples):
    range_len = samples.shape[2]
    flat = samples.reshape(samples.shape[0], 2 * range_len)
    first = jnp.dot(cosine, flat, precision=lax.Precision.HIGHEST, preferred_element_type=jnp.float32)
    second = jnp.dot(sine, flat, precision=lax.Precision.HIGHEST, preferred_element_type=jnp.float32)
    first = first.reshape(-1, 2, range_len)
    second = second.reshape(-1, 2, range_len)
    real_part = first[:, 0] + second[:, 1]
    imag_part = first[:, 1] - second[:, 0]
    return jnp.stack([real_part, imag_part], axis=1)

def phase_table(level, half, role, beam_rows, range_len):
    beam_ids = beam_rows[:, None] + 1
    range_ids = jnp.arange(range_len, dtype=jnp.int32)[None, :] + 1
    factor = 4 * level + 2 * half + role + 1
    turns = beam_ids * range_ids * factor % phase_modulus
    angle = turns.astype(jnp.float32) * (two_pi / phase_modulus)
    return (jnp.cos(angle), jnp.sin(angle))

def rotate(term, cosine, sine):
    real_part = cosine * term[:, 0] - sine * term[:, 1]
    imag_part = cosine * term[:, 1] + sine * term[:, 0]
    return jnp.stack([real_part, imag_part], axis=1)

def reference(pulses, owners, interp, pattern):
    owner_list = owners[:, 0]
    order = jnp.argsort(owner_list, stable=True).astype(jnp.int32)
    most = N_SUB * N_BEAM * CAP
    owner_device_index = jnp.arange(N_SUB, dtype=jnp.int32)
    counts = lax.optimization_barrier(jnp.sum((owner_list[None, :] == owner_device_index[:, None]).astype(jnp.int32), axis=1))
    starts = (jnp.cumsum(counts) - counts).astype(jnp.int32)
    padded_order = jnp.concatenate([order, jnp.zeros((most,), jnp.int32)])
    beam_rows = jnp.arange(BEAMS, dtype=jnp.int32)
    scale = 1.0 / math.sqrt(P_DEV * N_BEAM)

    def one_owner(owner):
        picked_samples = lax.dynamic_slice(padded_order, (starts[owner],), (most,))
        valid = jnp.arange(most, dtype=jnp.int32) < counts[owner]
        samples = jnp.where(valid[:, None, None], pulses[picked_samples], jnp.zeros((), pulses.dtype))
        cosine, sine = steer_terms(beam_rows, picked_samples, BEAMS)
        return (scale * beamform(cosine, sine, samples)).astype(jnp.bfloat16)
    image = lax.map(one_owner, owner_device_index)
    for level in range(LEVELS):
        bit = 1 << level
        tiles = image.reshape(N_SUB, TILES, TILE, 2 * RANGE)

        def interpolate(owner):
            role = owner >> level & 1
            interp_weight_table = interp[level][role].astype(jnp.float32)
            selected_entries = tiles[owner][pattern[level]].astype(jnp.float32)
            return jnp.einsum('jqab,jqbc->jac', interp_weight_table, selected_entries)
        terms = lax.map(interpolate, owner_device_index)

        def combine(owner):
            half = owner >> level & 1
            lower = owner - half * bit
            total = jnp.zeros((BEAMS, 2, RANGE), jnp.float32)
            for role in range(2):
                term = terms[lower + role * bit].reshape(BEAMS, 2, RANGE)
                cosine, sine = phase_table(level, half, role, beam_rows, RANGE)
                total = total + rotate(term, cosine, sine)
            return total.astype(jnp.bfloat16)
        image = lax.map(combine, owner_device_index)
    return image
```

```python
import functools
import math

import jax
import jax.numpy as jnp
import numpy as np
from jax import lax
from jax.experimental import pallas as pl
from jax.experimental.pallas import tpu as pltpu
from jax.sharding import PartitionSpec as P

two_pi = 2.0 * math.pi
phase_modulus = 1021


def partner_2(block, axis, bit):
    count = lax.axis_size(axis)
    route = []
    for low in range(count):
        high = low | 1 << bit
        if high != low and high < count:
            route += [(low, high), (high, low)]
    return lax.ppermute(block, axis, route)


def steer_terms(beam_rows, sample_positions, beam_count):
    turns = beam_rows[:, None] * sample_positions[None, :] % beam_count
    angle = turns.astype(jnp.float32) * (two_pi / beam_count)
    return (jnp.cos(angle), jnp.sin(angle))


def beamform(cosine, sine, samples):
    range_len = samples.shape[2]
    flat = samples.reshape(samples.shape[0], 2 * range_len)
    first = jnp.dot(
        cosine, flat, precision=lax.Precision.HIGHEST, preferred_element_type=jnp.float32
    )
    second = jnp.dot(
        sine, flat, precision=lax.Precision.HIGHEST, preferred_element_type=jnp.float32
    )
    first = first.reshape(-1, 2, range_len)
    second = second.reshape(-1, 2, range_len)
    real_part = first[:, 0] + second[:, 1]
    imag_part = first[:, 1] - second[:, 0]
    return jnp.stack([real_part, imag_part], axis=1)


def phase_table(level, half, role, beam_rows, range_len):
    beam_ids = beam_rows[:, None] + 1
    range_ids = jnp.arange(range_len, dtype=jnp.int32)[None, :] + 1
    factor = 4 * level + 2 * half + role + 1
    turns = beam_ids * range_ids * factor % phase_modulus
    angle = turns.astype(jnp.float32) * (two_pi / phase_modulus)
    return (jnp.cos(angle), jnp.sin(angle))


def rotate(term, cosine, sine):
    real_part = cosine * term[:, 0] - sine * term[:, 1]
    imag_part = cosine * term[:, 1] + sine * term[:, 0]
    return jnp.stack([real_part, imag_part], axis=1)


def local_general(pulses, owners, interp, pattern):
    sub_count = lax.axis_size("sub")
    beam_count = lax.axis_size("beam")
    sub_index = lax.axis_index("sub")
    beam_index = lax.axis_index("beam")
    pulse_count = pulses.shape[0]
    range_len = pulses.shape[2]
    levels = interp.shape[0]
    tiles_here = interp.shape[2]
    tile_row_block = interp.shape[-1]
    beam_here = tiles_here * tile_row_block
    beam_total = beam_here * beam_count
    capacity = max(2, 2 * pulse_count // sub_count)
    slot_total = sub_count * capacity
    owner_list = owners[:, 0]
    member = (owner_list[:, None] == jnp.arange(sub_count, dtype=jnp.int32)[None, :]).astype(
        jnp.int32
    )
    earlier = jnp.cumsum(member, axis=0) - member
    slot_rank = jnp.sum(earlier * member, axis=1)
    target = owner_list * capacity + slot_rank
    placing = (target[None, :] == jnp.arange(slot_total, dtype=jnp.int32)[:, None]).astype(
        jnp.float32
    )
    device_rank = sub_index * beam_count + beam_index
    sample_positions = (
        device_rank * pulse_count + jnp.arange(pulse_count, dtype=jnp.int32)
    ).astype(jnp.float32)
    send_samples = jnp.dot(
        placing,
        pulses.reshape(pulse_count, 2 * range_len),
        precision=lax.Precision.HIGHEST,
        preferred_element_type=jnp.float32,
    )
    send_samples = send_samples.reshape(sub_count, capacity, 2, range_len)
    send_positions = jnp.dot(
        placing,
        sample_positions,
        precision=lax.Precision.HIGHEST,
        preferred_element_type=jnp.float32,
    )
    send_positions = send_positions.reshape(sub_count, capacity)
    got_samples, got_positions = (
        lax.all_to_all(send_samples, "sub", split_axis=0, concat_axis=0, tiled=True),
        lax.all_to_all(send_positions, "sub", split_axis=0, concat_axis=0, tiled=True),
    )
    got_samples = got_samples.reshape(slot_total, 2, range_len)
    got_positions = got_positions.reshape(slot_total)
    scale = 1.0 / math.sqrt(pulse_count * beam_count)
    my_rows = beam_index * beam_here + jnp.arange(beam_here, dtype=jnp.int32)
    slot_positions = got_positions.astype(jnp.int32)
    rows = jnp.arange(beam_here * lax.axis_size("beam"), dtype=jnp.int32)
    partial_cosine, partial_sine = steer_terms(rows, slot_positions, beam_total)
    base = lax.psum_scatter(
        beamform(partial_cosine, partial_sine, got_samples), "beam", scatter_dimension=0, tiled=True
    )
    image = (scale * base).astype(jnp.bfloat16)
    for level in range(levels):
        half = sub_index >> level & 1
        local_access_pattern = lax.dynamic_slice_in_dim(
            pattern[level], beam_index * tiles_here, tiles_here, 0
        )
        own_weights = lax.dynamic_index_in_dim(interp[level], half, 0, keepdims=False)
        other_weights = lax.dynamic_index_in_dim(interp[level], 1 - half, 0, keepdims=False)

        def taps_sum(interp_weight_table, piece):
            piece_tiles = piece.reshape(-1, tile_row_block, 2 * range_len)
            tile_count = piece_tiles.shape[0]
            inside = (local_access_pattern >= 0) & (local_access_pattern < tile_count)
            selected_entries = piece_tiles[jnp.clip(local_access_pattern, 0, tile_count - 1)]
            selected_entries = jnp.where(
                inside[:, :, None, None], selected_entries, jnp.zeros((), jnp.bfloat16)
            )
            return jnp.einsum(
                "jvlx,jvxu->jlu",
                interp_weight_table,
                selected_entries,
                preferred_element_type=jnp.float32,
            )

        partner = partner_2(image, "sub", level)
        local_term_value = taps_sum(own_weights, lax.all_gather(image, "beam", axis=0, tiled=True))
        other_term = taps_sum(other_weights, lax.all_gather(partner, "beam", axis=0, tiled=True))
        merged = jnp.zeros((beam_here, 2, range_len), jnp.float32)
        for term_part, role in ((local_term_value, half), (other_term, 1 - half)):
            term = term_part.reshape(beam_here, 2, range_len)
            cosine, sine = phase_table(level, half, role, my_rows, range_len)
            merged = merged + rotate(term, cosine, sine)
        image = merged.astype(jnp.bfloat16)
    return image[None]


MESH = pl.DeviceIdType.MESH


def kernel(
    dims, x_ref, own_ref, interp_ref, pattern_ref, steer_ref, phase_ref, out_ref,
    got, got_own, weights, sums, turns, image, term, send, landed,
    pulse_send, pulse_recv, own_send, own_recv, weight_send, weight_recv, out_send, out_recv,
):
    subs, beams, ranges, tile, levels, scale = dims
    count = subs * beams
    rows = 2 * ranges
    group = lax.axis_index("groups")
    beam = lax.axis_index("beam")
    me = lax.axis_index("sub") * beams + beam

    def place(peer):
        return (group, peer // beams, peer % beams)

    def ahead(step):
        return lax.rem(me + step, count)

    barrier = pltpu.get_barrier_semaphore()
    for step in range(1, count):
        pl.semaphore_signal(barrier, inc=1, device_id=place(ahead(step)), device_id_type=MESH)
    pl.semaphore_wait(barrier, count - 1)

    pulse_copies, own_copies = [None], [None]
    for step in range(1, count):
        own_copy = pltpu.make_async_remote_copy(
            src_ref=own_ref, dst_ref=got_own.at[step],
            send_sem=own_send.at[step], recv_sem=own_recv.at[step],
            device_id=place(ahead(step)), device_id_type=MESH,
        )
        own_copy.start()
        own_copies.append(own_copy)
        copy = pltpu.make_async_remote_copy(
            src_ref=x_ref.at[ahead(step)], dst_ref=got.at[step],
            send_sem=pulse_send.at[step], recv_sem=pulse_recv.at[step],
            device_id=place(ahead(step)), device_id_type=MESH,
        )
        copy.start()
        pulse_copies.append(copy)

    def beam_at(slot):
        return lax.rem(beam // 2 + slot // 2, 2) * 2 + lax.rem(beam % 2 + slot % 2, 2)

    def weight_copy(source, slot, toward):
        return pltpu.make_async_remote_copy(
            src_ref=source, dst_ref=weights.at[slot],
            send_sem=weight_send.at[slot], recv_sem=weight_recv.at[slot],
            device_id=(group, lax.axis_index("sub"), beam_at(toward)), device_id_type=MESH,
        )

    across = weight_copy(interp_ref, 2, 2)
    across.start()
    beside = weight_copy(interp_ref, 1, 1)
    beside.start()

    first_cos = phase_ref[me, 0]
    first_sin = phase_ref[me, 1]
    power_cos, power_sin = first_cos, first_sin
    for power in range(4 * levels):
        if power:
            power_cos, power_sin = (
                power_cos * first_cos - power_sin * first_sin,
                power_cos * first_sin + power_sin * first_cos,
            )
        turns[power, 0] = power_cos
        turns[power, 1] = power_sin

    def add_in(values, owner_row, begin):
        wide = values.astype(jnp.float32)
        for owner in range(subs):
            part = jnp.where(owner_row == owner, wide, 0.0)
            at = pl.ds(owner * rows, rows)
            sums[at, :] = part if begin else sums[at, :] + part

    add_in(x_ref[me], own_ref[...], True)

    across.wait_recv()
    passed_on = weight_copy(weights.at[2], 3, 1)
    passed_on.start()

    for step in range(1, count):
        own_copies[step].wait_recv()
        pulse_copies[step].wait_recv()
        add_in(got[step], got_own[step], False)

    turned = jnp.dot(
        sums[...].astype(jnp.bfloat16), steer_ref[...], preferred_element_type=jnp.float32
    )
    width = turned.shape[1] // 2
    tiles = width // tile

    def members(level, half):
        return [s for s in range(subs) if s >> level & 1 == half]

    def keep(level, owner, block, value):
        half = owner >> level & 1
        at = members(level, half).index(owner) * rows
        image[block, half, at : at + rows, :] = value

    for owner in range(subs):
        part = turned[owner * rows : (owner + 1) * rows]
        real = part[:ranges, :width] + part[ranges:, width:]
        imag = part[ranges:, :width] - part[:ranges, width:]
        base = (scale * jnp.concatenate([real, imag], axis=0)).astype(jnp.bfloat16)
        for block in range(tiles):
            keep(0, owner, block, base[:, block * tile : (block + 1) * tile])

    beside.wait_recv()
    passed_on.wait_recv()

    out_copies = []
    for level in range(levels):
        bit = 1 << level
        for slot in range(tiles):
            block = beam_at(slot)
            for half in range(2):
                value = None
                for tap in range(2):
                    kernel_here = (
                        interp_ref[level, half, 0, tap]
                        if slot == 0
                        else weights[slot, level, half, 0, tap]
                    )
                    child = image[pattern_ref[level, block, tap], half]
                    product = lax.dot_general(
                        child, kernel_here, (((1,), (1,)), ((), ())),
                        preferred_element_type=jnp.float32,
                    )
                    value = product if value is None else value + product
                term[block, half] = value
        for owner in range(subs):
            half = owner >> level & 1
            for block in range(tiles):
                real = imag = 0.0
                for role in range(2):
                    child = owner - half * bit + role * bit
                    at = members(level, role).index(child) * rows
                    power = 4 * level + 2 * half + role
                    lanes = pl.ds(block * tile, tile)
                    cosine = turns[power, 0, :, lanes]
                    sine = turns[power, 1, :, lanes]
                    child_real = term[block, role, at : at + ranges, :]
                    child_imag = term[block, role, at + ranges : at + rows, :]
                    real = real + (cosine * child_real - sine * child_imag)
                    imag = imag + (cosine * child_imag + sine * child_real)
                merged = jnp.concatenate([real, imag], axis=0).astype(jnp.bfloat16)
                if level < levels - 1:
                    keep(level + 1, owner, block, merged)
                else:
                    send[owner * beams + block] = merged

    for step in range(1, count):
        copy = pltpu.make_async_remote_copy(
            src_ref=send.at[ahead(step)], dst_ref=landed.at[step],
            send_sem=out_send.at[step], recv_sem=out_recv.at[step],
            device_id=place(ahead(step)), device_id_type=MESH,
        )
        copy.start()
        out_copies.append(copy)
    out_ref[me] = send[me]
    for step in range(1, count):
        out_copies[step - 1].wait_recv()
        out_ref[lax.rem(me + count - step, count)] = landed[step]
    for step in range(1, count):
        out_copies[step - 1].wait_send()
        pulse_copies[step].wait_send()
        own_copies[step].wait_send()
    across.wait_send()
    beside.wait_send()
    passed_on.wait_send()


def local_sliced(pulses, owners, interp, pattern, *, subs, beams):
    pulse_count, _, range_len = pulses.shape
    levels, _, _, taps, tile, _ = interp.shape
    count = subs * beams
    ranges = range_len // count
    rows = 2 * ranges
    width = beams * tile
    x = pulses.astype(jnp.bfloat16).reshape(pulse_count, 2, count, ranges)
    x = x.transpose(2, 1, 3, 0).reshape(count, rows, pulse_count)
    angle = two_pi / width * (np.arange(pulse_count)[:, None] * np.arange(width)[None, :] % width)
    steer = np.concatenate([np.cos(angle), np.sin(angle)], axis=1).astype(jnp.bfloat16)
    beam_ids = np.arange(width)[None, :] + 1
    range_ids = np.arange(range_len)[:, None] + 1
    phase = two_pi / phase_modulus * (beam_ids * range_ids % phase_modulus)
    phase = np.stack([np.cos(phase), np.sin(phase)], axis=0).astype(np.float32)
    phase = phase.reshape(2, count, ranges, width).transpose(1, 0, 2, 3)
    scale = 1.0 / math.sqrt(pulse_count * beams)
    vmem = pl.BlockSpec(memory_space=pltpu.VMEM)
    out = pl.pallas_call(
        functools.partial(kernel, (subs, beams, ranges, tile, levels, scale)),
        out_shape=jax.ShapeDtypeStruct((count, rows, tile), jnp.bfloat16),
        in_specs=[vmem, vmem, vmem, pl.BlockSpec(memory_space=pltpu.SMEM), vmem, vmem],
        out_specs=vmem,
        scratch_shapes=[
            pltpu.VMEM((count, rows, pulse_count), jnp.bfloat16),
            pltpu.VMEM((count, 1, pulse_count), jnp.int32),
            pltpu.VMEM((4,) + interp.shape, jnp.bfloat16),
            pltpu.VMEM((subs * rows, pulse_count), jnp.float32),
            pltpu.VMEM((4 * levels, 2, ranges, width), jnp.float32),
            pltpu.VMEM((beams, 2, subs // 2 * rows, tile), jnp.bfloat16),
            pltpu.VMEM((beams, 2, subs // 2 * rows, tile), jnp.float32),
            pltpu.VMEM((count, rows, tile), jnp.bfloat16),
            pltpu.VMEM((count, rows, tile), jnp.bfloat16),
        ]
        + [pltpu.SemaphoreType.DMA((count,))] * 4
        + [pltpu.SemaphoreType.DMA((4,))] * 2
        + [pltpu.SemaphoreType.DMA((count,))] * 2,
        compiler_params=pltpu.CompilerParams(
            collective_id=0, has_side_effects=True, vmem_limit_bytes=40 * 2**20
        ),
    )(x, owners.reshape(1, pulse_count), interp, pattern, steer, phase)
    out = out.reshape(count, 2, ranges, tile).transpose(3, 1, 0, 2)
    return out.reshape(1, tile, 2, range_len)


def solution(mesh):
    subs, beams = mesh.shape["sub"], mesh.shape["beam"]

    def local(pulses, owners, interp, pattern):
        pulse_count, _, range_len = pulses.shape
        levels, _, tiles_here, taps, tile, _ = interp.shape
        if (
            range_len % (8 * subs * beams) == 0
            and beams == 4
            and subs == 1 << levels
            and tiles_here == 1
            and taps == 2
            and pulse_count % (beams * tile) == 0
            and tile % 128 == 0
        ):
            return local_sliced(pulses, owners, interp, pattern, subs=subs, beams=beams)
        return local_general(pulses, owners, interp, pattern)

    in_specs = (
        P(("groups", "sub", "beam"), None, None),
        P(("groups", "sub", "beam"), None),
        P(None, None, "beam", None, None, None),
        P(),
    )
    out_specs = P(("groups", "sub"), "beam", None, None)
    return jax.shard_map(local, mesh=mesh, in_specs=in_specs, out_specs=out_specs, check_vma=False)
```

```python
import functools
import math

import jax
import jax.numpy as jnp
import numpy as np
from jax import lax
from jax.experimental import pallas as pl
from jax.experimental.pallas import tpu as pltpu
from jax.sharding import PartitionSpec as P

two_pi = 2.0 * math.pi
phase_modulus = 1021


def partner_2(block, axis, bit):
    count = lax.axis_size(axis)
    route = []
    for low in range(count):
        high = low | 1 << bit
        if high != low and high < count:
            route += [(low, high), (high, low)]
    return lax.ppermute(block, axis, route)


def steer_terms(beam_rows, sample_positions, beam_count):
    turns = beam_rows[:, None] * sample_positions[None, :] % beam_count
    angle = turns.astype(jnp.float32) * (two_pi / beam_count)
    return (jnp.cos(angle), jnp.sin(angle))


def beamform(cosine, sine, samples):
    range_len = samples.shape[2]
    flat = samples.reshape(samples.shape[0], 2 * range_len)
    first = jnp.dot(
        cosine, flat, precision=lax.Precision.HIGHEST, preferred_element_type=jnp.float32
    )
    second = jnp.dot(
        sine, flat, precision=lax.Precision.HIGHEST, preferred_element_type=jnp.float32
    )
    first = first.reshape(-1, 2, range_len)
    second = second.reshape(-1, 2, range_len)
    real_part = first[:, 0] + second[:, 1]
    imag_part = first[:, 1] - second[:, 0]
    return jnp.stack([real_part, imag_part], axis=1)


def phase_table(level, half, role, beam_rows, range_len):
    beam_ids = beam_rows[:, None] + 1
    range_ids = jnp.arange(range_len, dtype=jnp.int32)[None, :] + 1
    factor = 4 * level + 2 * half + role + 1
    turns = beam_ids * range_ids * factor % phase_modulus
    angle = turns.astype(jnp.float32) * (two_pi / phase_modulus)
    return (jnp.cos(angle), jnp.sin(angle))


def rotate(term, cosine, sine):
    real_part = cosine * term[:, 0] - sine * term[:, 1]
    imag_part = cosine * term[:, 1] + sine * term[:, 0]
    return jnp.stack([real_part, imag_part], axis=1)


def local_general(pulses, owners, interp, pattern):
    sub_count = lax.axis_size("sub")
    beam_count = lax.axis_size("beam")
    sub_index = lax.axis_index("sub")
    beam_index = lax.axis_index("beam")
    pulse_count = pulses.shape[0]
    range_len = pulses.shape[2]
    levels = interp.shape[0]
    tiles_here = interp.shape[2]
    tile_row_block = interp.shape[-1]
    beam_here = tiles_here * tile_row_block
    beam_total = beam_here * beam_count
    capacity = max(2, 2 * pulse_count // sub_count)
    slot_total = sub_count * capacity
    owner_list = owners[:, 0]
    member = (owner_list[:, None] == jnp.arange(sub_count, dtype=jnp.int32)[None, :]).astype(
        jnp.int32
    )
    earlier = jnp.cumsum(member, axis=0) - member
    slot_rank = jnp.sum(earlier * member, axis=1)
    target = owner_list * capacity + slot_rank
    placing = (target[None, :] == jnp.arange(slot_total, dtype=jnp.int32)[:, None]).astype(
        jnp.float32
    )
    device_rank = sub_index * beam_count + beam_index
    sample_positions = (
        device_rank * pulse_count + jnp.arange(pulse_count, dtype=jnp.int32)
    ).astype(jnp.float32)
    send_samples = jnp.dot(
        placing,
        pulses.reshape(pulse_count, 2 * range_len),
        precision=lax.Precision.HIGHEST,
        preferred_element_type=jnp.float32,
    )
    send_samples = send_samples.reshape(sub_count, capacity, 2, range_len)
    send_positions = jnp.dot(
        placing,
        sample_positions,
        precision=lax.Precision.HIGHEST,
        preferred_element_type=jnp.float32,
    )
    send_positions = send_positions.reshape(sub_count, capacity)
    got_samples, got_positions = (
        lax.all_to_all(send_samples, "sub", split_axis=0, concat_axis=0, tiled=True),
        lax.all_to_all(send_positions, "sub", split_axis=0, concat_axis=0, tiled=True),
    )
    got_samples = got_samples.reshape(slot_total, 2, range_len)
    got_positions = got_positions.reshape(slot_total)
    scale = 1.0 / math.sqrt(pulse_count * beam_count)
    my_rows = beam_index * beam_here + jnp.arange(beam_here, dtype=jnp.int32)
    slot_positions = got_positions.astype(jnp.int32)
    rows = jnp.arange(beam_here * lax.axis_size("beam"), dtype=jnp.int32)
    partial_cosine, partial_sine = steer_terms(rows, slot_positions, beam_total)
    base = lax.psum_scatter(
        beamform(partial_cosine, partial_sine, got_samples), "beam", scatter_dimension=0, tiled=True
    )
    image = (scale * base).astype(jnp.bfloat16)
    for level in range(levels):
        half = sub_index >> level & 1
        local_access_pattern = lax.dynamic_slice_in_dim(
            pattern[level], beam_index * tiles_here, tiles_here, 0
        )
        own_weights = lax.dynamic_index_in_dim(interp[level], half, 0, keepdims=False)
        other_weights = lax.dynamic_index_in_dim(interp[level], 1 - half, 0, keepdims=False)

        def taps_sum(interp_weight_table, piece):
            piece_tiles = piece.reshape(-1, tile_row_block, 2 * range_len)
            tile_count = piece_tiles.shape[0]
            inside = (local_access_pattern >= 0) & (local_access_pattern < tile_count)
            selected_entries = piece_tiles[jnp.clip(local_access_pattern, 0, tile_count - 1)]
            selected_entries = jnp.where(
                inside[:, :, None, None], selected_entries, jnp.zeros((), jnp.bfloat16)
            )
            return jnp.einsum(
                "jvlx,jvxu->jlu",
                interp_weight_table,
                selected_entries,
                preferred_element_type=jnp.float32,
            )

        partner = partner_2(image, "sub", level)
        local_term_value = taps_sum(own_weights, lax.all_gather(image, "beam", axis=0, tiled=True))
        other_term = taps_sum(other_weights, lax.all_gather(partner, "beam", axis=0, tiled=True))
        merged = jnp.zeros((beam_here, 2, range_len), jnp.float32)
        for term_part, role in ((local_term_value, half), (other_term, 1 - half)):
            term = term_part.reshape(beam_here, 2, range_len)
            cosine, sine = phase_table(level, half, role, my_rows, range_len)
            merged = merged + rotate(term, cosine, sine)
        image = merged.astype(jnp.bfloat16)
    return image[None]


MESH = pl.DeviceIdType.MESH


def kernel(
    dims, raw_ref, own_ref, interp_ref, pattern_ref, steer_ref, phase_ref, out_ref,
    raw, spread, pieces, steer, phase, got, got_own, weights, sums, turns, image, term, send, landed,
    local_sem, pulse_send, pulse_recv, own_send, own_recv, weight_send, weight_recv, out_send, out_recv,
):
    subs, beams, ranges, tile, levels, scale = dims
    count = subs * beams
    rows = 2 * ranges
    group = lax.axis_index("groups")
    beam = lax.axis_index("beam")
    me = lax.axis_index("sub") * beams + beam

    def place(peer):
        return (group, peer // beams, peer % beams)

    def ahead(step):
        return lax.rem(me + step, count)

    barrier = pltpu.get_barrier_semaphore()
    for step in range(1, count):
        pl.semaphore_signal(barrier, inc=1, device_id=place(ahead(step)), device_id_type=MESH)

    staged = [
        pltpu.make_async_copy(source, target, local_sem.at[number])
        for number, (source, target) in enumerate(
            [
                (raw_ref, raw),
                (interp_ref, weights.at[0]),
                (own_ref, got_own.at[0]),
                (phase_ref.at[me], phase),
                (steer_ref, steer),
            ]
        )
    ]
    for copy in staged:
        copy.start()

    span = spread.shape[1]
    lane_tiles = span // 128
    pulse_count = spread.shape[2]
    staged[0].wait()
    for lane_tile in range(lane_tiles):
        for part in range(2):
            block = raw[:, part, pl.ds(128 * lane_tile, 128)]
            spread[part, pl.ds(128 * lane_tile, 128), :] = block.T
    for piece in range(count):
        at = pl.ds(piece * ranges, ranges)
        both = jnp.concatenate([spread[0, at, :], spread[1, at, :]], axis=0)
        pieces[piece] = both.astype(jnp.bfloat16)
    for copy in staged[1:]:
        copy.wait()
    pl.semaphore_wait(barrier, count - 1)

    pulse_copies, own_copies = [None], [None]
    for step in range(1, count):
        own_copy = pltpu.make_async_remote_copy(
            src_ref=got_own.at[0], dst_ref=got_own.at[step],
            send_sem=own_send.at[step], recv_sem=own_recv.at[step],
            device_id=place(ahead(step)), device_id_type=MESH,
        )
        own_copy.start()
        own_copies.append(own_copy)
        copy = pltpu.make_async_remote_copy(
            src_ref=pieces.at[ahead(step)], dst_ref=got.at[step],
            send_sem=pulse_send.at[step], recv_sem=pulse_recv.at[step],
            device_id=place(ahead(step)), device_id_type=MESH,
        )
        copy.start()
        pulse_copies.append(copy)

    def beam_at(slot):
        return lax.rem(beam // 2 + slot // 2, 2) * 2 + lax.rem(beam % 2 + slot % 2, 2)

    def weight_copy(source, slot, toward):
        return pltpu.make_async_remote_copy(
            src_ref=source, dst_ref=weights.at[slot],
            send_sem=weight_send.at[slot], recv_sem=weight_recv.at[slot],
            device_id=(group, lax.axis_index("sub"), beam_at(toward)), device_id_type=MESH,
        )

    across = weight_copy(weights.at[0], 2, 2)
    across.start()
    beside = weight_copy(weights.at[0], 1, 1)
    beside.start()

    first_cos = phase[0]
    first_sin = phase[1]
    power_cos, power_sin = first_cos, first_sin
    for power in range(4 * levels):
        if power:
            power_cos, power_sin = (
                power_cos * first_cos - power_sin * first_sin,
                power_cos * first_sin + power_sin * first_cos,
            )
        turns[power, 0] = power_cos
        turns[power, 1] = power_sin

    def add_in(values, owner_row, begin):
        wide = values.astype(jnp.float32)
        for owner in range(subs):
            part = jnp.where(owner_row == owner, wide, 0.0)
            at = pl.ds(owner * rows, rows)
            sums[at, :] = part if begin else sums[at, :] + part

    add_in(pieces[me], got_own[0], True)

    across.wait_recv()
    passed_on = weight_copy(weights.at[2], 3, 1)
    passed_on.start()

    for step in range(1, count):
        own_copies[step].wait_recv()
        pulse_copies[step].wait_recv()
        add_in(got[step], got_own[step], False)

    turned = jnp.dot(
        sums[...].astype(jnp.bfloat16), steer[...], preferred_element_type=jnp.float32
    )
    width = turned.shape[1] // 2
    tiles = width // tile

    def members(level, half):
        return [s for s in range(subs) if s >> level & 1 == half]

    def keep(level, owner, block, value):
        half = owner >> level & 1
        at = members(level, half).index(owner) * rows
        image[block, half, at : at + rows, :] = value

    for owner in range(subs):
        part = turned[owner * rows : (owner + 1) * rows]
        real = part[:ranges, :width] + part[ranges:, width:]
        imag = part[ranges:, :width] - part[:ranges, width:]
        base = (scale * jnp.concatenate([real, imag], axis=0)).astype(jnp.bfloat16)
        for block in range(tiles):
            keep(0, owner, block, base[:, block * tile : (block + 1) * tile])

    beside.wait_recv()
    passed_on.wait_recv()

    out_copies = []
    for level in range(levels):
        bit = 1 << level
        for slot in range(tiles):
            block = beam_at(slot)
            for half in range(2):
                value = None
                for tap in range(2):
                    kernel_here = weights[slot, level, half, 0, tap]
                    child = image[pattern_ref[level, tap, block], half]
                    product = lax.dot_general(
                        child, kernel_here, (((1,), (1,)), ((), ())),
                        preferred_element_type=jnp.float32,
                    )
                    value = product if value is None else value + product
                term[block, half] = value
        for owner in range(subs):
            half = owner >> level & 1
            for block in range(tiles):
                real = imag = 0.0
                for role in range(2):
                    child = owner - half * bit + role * bit
                    at = members(level, role).index(child) * rows
                    power = 4 * level + 2 * half + role
                    lanes = pl.ds(block * tile, tile)
                    cosine = turns[power, 0, :, lanes]
                    sine = turns[power, 1, :, lanes]
                    child_real = term[block, role, at : at + ranges, :]
                    child_imag = term[block, role, at + ranges : at + rows, :]
                    real = real + (cosine * child_real - sine * child_imag)
                    imag = imag + (cosine * child_imag + sine * child_real)
                merged = jnp.concatenate([real, imag], axis=0).astype(jnp.bfloat16)
                if level < levels - 1:
                    keep(level + 1, owner, block, merged)
                else:
                    send[owner * beams + block] = merged

    for step in range(1, count):
        copy = pltpu.make_async_remote_copy(
            src_ref=send.at[ahead(step)], dst_ref=landed.at[me],
            send_sem=out_send.at[step], recv_sem=out_recv.at[me],
            device_id=place(ahead(step)), device_id_type=MESH,
        )
        copy.start()
        out_copies.append(copy)
    landed[me] = send[me]
    for step in range(1, count):
        source = ahead(count - step)
        pltpu.make_async_remote_copy(
            src_ref=send.at[source], dst_ref=landed.at[source],
            send_sem=out_send.at[step], recv_sem=out_recv.at[source],
            device_id=place(source), device_id_type=MESH,
        ).wait_recv()
    for part in range(2):
        strips = [landed[source].astype(jnp.float32) for source in range(count)]
        whole = [strip[part * ranges : (part + 1) * ranges] for strip in strips]
        out_ref[part] = jnp.concatenate(whole, axis=0).astype(jnp.bfloat16)
    for step in range(1, count):
        out_copies[step - 1].wait_send()
        pulse_copies[step].wait_send()
        own_copies[step].wait_send()
    across.wait_send()
    beside.wait_send()
    passed_on.wait_send()


def local_sliced(pulses, owners, interp, pattern, *, subs, beams):
    pulse_count, _, range_len = pulses.shape
    levels, _, _, taps, tile, _ = interp.shape
    count = subs * beams
    ranges = range_len // count
    rows = 2 * ranges
    width = beams * tile
    x = pulses
    angle = two_pi / width * (np.arange(pulse_count)[:, None] * np.arange(width)[None, :] % width)
    steer = np.concatenate([np.cos(angle), np.sin(angle)], axis=1).astype(jnp.bfloat16)
    beam_ids = np.arange(width)[None, :] + 1
    range_ids = np.arange(range_len)[:, None] + 1
    phase = two_pi / phase_modulus * (beam_ids * range_ids % phase_modulus)
    phase = np.stack([np.cos(phase), np.sin(phase)], axis=0).astype(np.float32)
    phase = phase.reshape(2, count, ranges, width).transpose(1, 0, 2, 3)
    scale = 1.0 / math.sqrt(pulse_count * beams)
    vmem = pl.BlockSpec(memory_space=pltpu.VMEM)
    hbm = pl.BlockSpec(memory_space=pltpu.HBM)
    out = pl.pallas_call(
        functools.partial(kernel, (subs, beams, ranges, tile, levels, scale)),
        out_shape=jax.ShapeDtypeStruct((2, range_len, tile), jnp.bfloat16),
        in_specs=[hbm, hbm, hbm, pl.BlockSpec(memory_space=pltpu.SMEM), hbm, hbm],
        out_specs=vmem,
        scratch_shapes=[
            pltpu.VMEM(x.shape, jnp.float32),
            pltpu.VMEM((2, range_len, pulse_count), jnp.float32),
            pltpu.VMEM((count, rows, pulse_count), jnp.bfloat16),
            pltpu.VMEM(steer.shape, jnp.bfloat16),
            pltpu.VMEM(phase.shape[1:], jnp.float32),
            pltpu.VMEM((count, rows, pulse_count), jnp.bfloat16),
            pltpu.VMEM((count, 1, pulse_count), jnp.int32),
            pltpu.VMEM((4,) + interp.shape, jnp.bfloat16),
            pltpu.VMEM((subs * rows, pulse_count), jnp.float32),
            pltpu.VMEM((4 * levels, 2, ranges, width), jnp.float32),
            pltpu.VMEM((beams, 2, subs // 2 * rows, tile), jnp.bfloat16),
            pltpu.VMEM((beams, 2, subs // 2 * rows, tile), jnp.float32),
            pltpu.VMEM((count, rows, tile), jnp.bfloat16),
            pltpu.VMEM((count, rows, tile), jnp.bfloat16),
        ]
        + [pltpu.SemaphoreType.DMA((5,))]
        + [pltpu.SemaphoreType.DMA((count,))] * 4
        + [pltpu.SemaphoreType.DMA((4,))] * 2
        + [pltpu.SemaphoreType.DMA((count,))] * 2,
        compiler_params=pltpu.CompilerParams(
            collective_id=0, has_side_effects=True, vmem_limit_bytes=62 * 2**20
        ),
    )(x, owners.reshape(1, pulse_count), interp, pattern.transpose(0, 2, 1), steer, phase)
    return out.transpose(2, 0, 1)[None]


def solution(mesh):
    subs, beams = mesh.shape["sub"], mesh.shape["beam"]

    def local(pulses, owners, interp, pattern):
        pulse_count, _, range_len = pulses.shape
        levels, _, tiles_here, taps, tile, _ = interp.shape
        if (
            range_len % (8 * subs * beams) == 0
            and range_len % 128 == 0
            and beams == 4
            and subs == 1 << levels
            and tiles_here == 1
            and taps == 2
            and pulse_count % (beams * tile) == 0
            and tile % 128 == 0
        ):
            return local_sliced(pulses, owners, interp, pattern, subs=subs, beams=beams)
        return local_general(pulses, owners, interp, pattern)

    in_specs = (
        P(("groups", "sub", "beam"), None, None),
        P(("groups", "sub", "beam"), None),
        P(None, None, "beam", None, None, None),
        P(),
    )
    out_specs = P(("groups", "sub"), "beam", None, None)
    return jax.shard_map(local, mesh=mesh, in_specs=in_specs, out_specs=out_specs, check_vma=False)
```

```python
import functools
import math

import jax
import jax.numpy as jnp
import numpy as np
from jax import lax
from jax.experimental import pallas as pl
from jax.experimental.pallas import tpu as pltpu
from jax.sharding import PartitionSpec as P

two_pi = 2.0 * math.pi
phase_modulus = 1021


def partner_2(block, axis, bit):
    count = lax.axis_size(axis)
    route = []
    for low in range(count):
        high = low | 1 << bit
        if high != low and high < count:
            route += [(low, high), (high, low)]
    return lax.ppermute(block, axis, route)


def steer_terms(beam_rows, sample_positions, beam_count):
    turns = beam_rows[:, None] * sample_positions[None, :] % beam_count
    angle = turns.astype(jnp.float32) * (two_pi / beam_count)
    return (jnp.cos(angle), jnp.sin(angle))


def beamform(cosine, sine, samples):
    range_len = samples.shape[2]
    flat = samples.reshape(samples.shape[0], 2 * range_len)
    first = jnp.dot(
        cosine, flat, precision=lax.Precision.HIGHEST, preferred_element_type=jnp.float32
    )
    second = jnp.dot(
        sine, flat, precision=lax.Precision.HIGHEST, preferred_element_type=jnp.float32
    )
    first = first.reshape(-1, 2, range_len)
    second = second.reshape(-1, 2, range_len)
    real_part = first[:, 0] + second[:, 1]
    imag_part = first[:, 1] - second[:, 0]
    return jnp.stack([real_part, imag_part], axis=1)


def phase_table(level, half, role, beam_rows, range_len):
    beam_ids = beam_rows[:, None] + 1
    range_ids = jnp.arange(range_len, dtype=jnp.int32)[None, :] + 1
    factor = 4 * level + 2 * half + role + 1
    turns = beam_ids * range_ids * factor % phase_modulus
    angle = turns.astype(jnp.float32) * (two_pi / phase_modulus)
    return (jnp.cos(angle), jnp.sin(angle))


def rotate(term, cosine, sine):
    real_part = cosine * term[:, 0] - sine * term[:, 1]
    imag_part = cosine * term[:, 1] + sine * term[:, 0]
    return jnp.stack([real_part, imag_part], axis=1)


def local_general(pulses, owners, interp, pattern):
    sub_count = lax.axis_size("sub")
    beam_count = lax.axis_size("beam")
    sub_index = lax.axis_index("sub")
    beam_index = lax.axis_index("beam")
    pulse_count = pulses.shape[0]
    range_len = pulses.shape[2]
    levels = interp.shape[0]
    tiles_here = interp.shape[2]
    tile_row_block = interp.shape[-1]
    beam_here = tiles_here * tile_row_block
    beam_total = beam_here * beam_count
    capacity = max(2, 2 * pulse_count // sub_count)
    slot_total = sub_count * capacity
    owner_list = owners[:, 0]
    member = (owner_list[:, None] == jnp.arange(sub_count, dtype=jnp.int32)[None, :]).astype(
        jnp.int32
    )
    earlier = jnp.cumsum(member, axis=0) - member
    slot_rank = jnp.sum(earlier * member, axis=1)
    target = owner_list * capacity + slot_rank
    placing = (target[None, :] == jnp.arange(slot_total, dtype=jnp.int32)[:, None]).astype(
        jnp.float32
    )
    device_rank = sub_index * beam_count + beam_index
    sample_positions = (
        device_rank * pulse_count + jnp.arange(pulse_count, dtype=jnp.int32)
    ).astype(jnp.float32)
    send_samples = jnp.dot(
        placing,
        pulses.reshape(pulse_count, 2 * range_len),
        precision=lax.Precision.HIGHEST,
        preferred_element_type=jnp.float32,
    )
    send_samples = send_samples.reshape(sub_count, capacity, 2, range_len)
    send_positions = jnp.dot(
        placing,
        sample_positions,
        precision=lax.Precision.HIGHEST,
        preferred_element_type=jnp.float32,
    )
    send_positions = send_positions.reshape(sub_count, capacity)
    got_samples, got_positions = (
        lax.all_to_all(send_samples, "sub", split_axis=0, concat_axis=0, tiled=True),
        lax.all_to_all(send_positions, "sub", split_axis=0, concat_axis=0, tiled=True),
    )
    got_samples = got_samples.reshape(slot_total, 2, range_len)
    got_positions = got_positions.reshape(slot_total)
    scale = 1.0 / math.sqrt(pulse_count * beam_count)
    my_rows = beam_index * beam_here + jnp.arange(beam_here, dtype=jnp.int32)
    slot_positions = got_positions.astype(jnp.int32)
    rows = jnp.arange(beam_here * lax.axis_size("beam"), dtype=jnp.int32)
    partial_cosine, partial_sine = steer_terms(rows, slot_positions, beam_total)
    base = lax.psum_scatter(
        beamform(partial_cosine, partial_sine, got_samples), "beam", scatter_dimension=0, tiled=True
    )
    image = (scale * base).astype(jnp.bfloat16)
    for level in range(levels):
        half = sub_index >> level & 1
        local_access_pattern = lax.dynamic_slice_in_dim(
            pattern[level], beam_index * tiles_here, tiles_here, 0
        )
        own_weights = lax.dynamic_index_in_dim(interp[level], half, 0, keepdims=False)
        other_weights = lax.dynamic_index_in_dim(interp[level], 1 - half, 0, keepdims=False)

        def taps_sum(interp_weight_table, piece):
            piece_tiles = piece.reshape(-1, tile_row_block, 2 * range_len)
            tile_count = piece_tiles.shape[0]
            inside = (local_access_pattern >= 0) & (local_access_pattern < tile_count)
            selected_entries = piece_tiles[jnp.clip(local_access_pattern, 0, tile_count - 1)]
            selected_entries = jnp.where(
                inside[:, :, None, None], selected_entries, jnp.zeros((), jnp.bfloat16)
            )
            return jnp.einsum(
                "jvlx,jvxu->jlu",
                interp_weight_table,
                selected_entries,
                preferred_element_type=jnp.float32,
            )

        partner = partner_2(image, "sub", level)
        local_term_value = taps_sum(own_weights, lax.all_gather(image, "beam", axis=0, tiled=True))
        other_term = taps_sum(other_weights, lax.all_gather(partner, "beam", axis=0, tiled=True))
        merged = jnp.zeros((beam_here, 2, range_len), jnp.float32)
        for term_part, role in ((local_term_value, half), (other_term, 1 - half)):
            term = term_part.reshape(beam_here, 2, range_len)
            cosine, sine = phase_table(level, half, role, my_rows, range_len)
            merged = merged + rotate(term, cosine, sine)
        image = merged.astype(jnp.bfloat16)
    return image[None]


MESH = pl.DeviceIdType.MESH


def kernel(
    dims, raw_ref, own_ref, interp_ref, pattern_ref, steer_ref, phase_ref, out_ref,
    raw, spread, pieces, steer, phase, got, got_own, weights, sums, far_sums, far_out, far_in, summed, turns, image, term, send, landed,
    local_sem, pulse_send, pulse_recv, own_send, own_recv, weight_send, weight_recv, out_send, out_recv, sum_send, sum_recv,
):
    subs, beams, ranges, tile, levels, scale = dims
    count = subs * beams
    rows = 2 * ranges
    group = lax.axis_index("groups")
    beam = lax.axis_index("beam")
    me = lax.axis_index("sub") * beams + beam

    def place(peer):
        return (group, peer // beams, peer % beams)

    def ahead(step):
        return lax.rem(me + step, count)

    barrier = pltpu.get_barrier_semaphore()
    for step in range(1, count):
        pl.semaphore_signal(barrier, inc=1, device_id=place(ahead(step)), device_id_type=MESH)

    staged = [
        pltpu.make_async_copy(source, target, local_sem.at[number])
        for number, (source, target) in enumerate(
            [
                (raw_ref, raw),
                (interp_ref, weights.at[0]),
                (own_ref, got_own.at[0]),
                (phase_ref.at[me], phase),
                (steer_ref, steer),
            ]
        )
    ]
    for copy in staged:
        copy.start()

    span = spread.shape[1]
    lane_tiles = span // 128
    pulse_count = spread.shape[2]
    staged[0].wait()
    for lane_tile in range(lane_tiles):
        for part in range(2):
            block = raw[:, part, pl.ds(128 * lane_tile, 128)]
            spread[part, pl.ds(128 * lane_tile, 128), :] = block.T
    for piece in range(count):
        at = pl.ds(piece * ranges, ranges)
        both = jnp.concatenate([spread[0, at, :], spread[1, at, :]], axis=0)
        pieces[piece] = both.astype(jnp.bfloat16)
    for copy in staged[1:]:
        copy.wait()
    pl.semaphore_wait(barrier, count - 1)

    half_count = count // 2
    base_peer = me // half_count * half_count
    far = ahead(half_count)
    far_base = half_count - base_peer

    def beside_me(step):
        return lax.rem(me - base_peer + step, half_count)

    def pulse_copy(piece, slot, peer):
        return pltpu.make_async_remote_copy(
            src_ref=pieces.at[piece], dst_ref=got.at[slot],
            send_sem=pulse_send.at[slot], recv_sem=pulse_recv.at[slot],
            device_id=place(peer), device_id_type=MESH,
        )

    own_copies, far_copies, near_copies = [None], [None], [None]
    for step in range(1, half_count):
        peer = base_peer + beside_me(step)
        own_copy = pltpu.make_async_remote_copy(
            src_ref=got_own.at[0], dst_ref=got_own.at[step],
            send_sem=own_send.at[step], recv_sem=own_recv.at[step],
            device_id=place(peer), device_id_type=MESH,
        )
        own_copy.start()
        own_copies.append(own_copy)
        far_copies.append(pulse_copy(far_base + beside_me(step), step, peer))
        far_copies[step].start()
    for step in range(1, half_count):
        peer = base_peer + beside_me(step)
        near_copies.append(pulse_copy(peer, half_count + step, peer))
        near_copies[step].start()

    def beam_at(slot):
        return lax.rem(beam // 2 + slot // 2, 2) * 2 + lax.rem(beam % 2 + slot % 2, 2)

    def weight_copy(source, slot, toward):
        return pltpu.make_async_remote_copy(
            src_ref=source, dst_ref=weights.at[slot],
            send_sem=weight_send.at[slot], recv_sem=weight_recv.at[slot],
            device_id=(group, lax.axis_index("sub"), beam_at(toward)), device_id_type=MESH,
        )

    across = weight_copy(weights.at[0], 2, 2)
    across.start()
    beside = weight_copy(weights.at[0], 1, 1)
    beside.start()

    first_cos = phase[0]
    first_sin = phase[1]
    power_cos, power_sin = first_cos, first_sin
    for power in range(4 * levels):
        if power:
            power_cos, power_sin = (
                power_cos * first_cos - power_sin * first_sin,
                power_cos * first_sin + power_sin * first_cos,
            )
        turns[power, 0] = power_cos
        turns[power, 1] = power_sin

    def add_in(total, values, owner_row, begin):
        wide = values.astype(jnp.float32)
        for owner in range(subs):
            part = jnp.where(owner_row == owner, wide, 0.0)
            total[owner] = part if begin else total[owner] + part

    add_in(far_sums, pieces[far], got_own[0], True)
    for step in range(1, half_count):
        own_copies[step].wait_recv()
        far_copies[step].wait_recv()
        add_in(far_sums, got[step], got_own[step], False)
    sum_copies = []
    for owner in range(subs):
        far_out[owner] = far_sums[owner].astype(jnp.bfloat16)
        sum_copy = pltpu.make_async_remote_copy(
            src_ref=far_out.at[owner], dst_ref=far_in.at[owner],
            send_sem=sum_send.at[owner], recv_sem=sum_recv.at[owner],
            device_id=place(far), device_id_type=MESH,
        )
        sum_copy.start()
        sum_copies.append(sum_copy)
    add_in(sums, pieces[me], got_own[0], True)

    across.wait_recv()
    passed_on = weight_copy(weights.at[2], 3, 1)
    passed_on.start()

    for step in range(1, half_count):
        near_copies[step].wait_recv()
        add_in(sums, got[half_count + step], got_own[step], False)
    for owner in range(subs):
        sum_copies[owner].wait_recv()
        summed[pl.ds(owner * rows, rows), :] = (
            sums[owner] + far_in[owner].astype(jnp.float32)
        ).astype(jnp.bfloat16)

    turned = jnp.dot(summed[...], steer[...], preferred_element_type=jnp.float32)
    width = turned.shape[1] // 2
    tiles = width // tile

    def members(level, half):
        return [s for s in range(subs) if s >> level & 1 == half]

    def keep(level, owner, block, value):
        half = owner >> level & 1
        at = members(level, half).index(owner) * rows
        image[block, half, at : at + rows, :] = value

    for owner in range(subs):
        part = turned[owner * rows : (owner + 1) * rows]
        real = part[:ranges, :width] + part[ranges:, width:]
        imag = part[ranges:, :width] - part[:ranges, width:]
        base = (scale * jnp.concatenate([real, imag], axis=0)).astype(jnp.bfloat16)
        for block in range(tiles):
            keep(0, owner, block, base[:, block * tile : (block + 1) * tile])

    beside.wait_recv()
    passed_on.wait_recv()

    out_copies = []
    for level in range(levels):
        bit = 1 << level
        for slot in range(tiles):
            block = beam_at(slot)
            for half in range(2):
                value = None
                for tap in range(2):
                    kernel_here = weights[slot, level, half, 0, tap]
                    child = image[pattern_ref[level, tap, block], half]
                    product = lax.dot_general(
                        child, kernel_here, (((1,), (1,)), ((), ())),
                        preferred_element_type=jnp.float32,
                    )
                    value = product if value is None else value + product
                term[block, half] = value
        for owner in range(subs):
            half = owner >> level & 1
            for block in range(tiles):
                real = imag = 0.0
                for role in range(2):
                    child = owner - half * bit + role * bit
                    at = members(level, role).index(child) * rows
                    power = 4 * level + 2 * half + role
                    lanes = pl.ds(block * tile, tile)
                    cosine = turns[power, 0, :, lanes]
                    sine = turns[power, 1, :, lanes]
                    child_real = term[block, role, at : at + ranges, :]
                    child_imag = term[block, role, at + ranges : at + rows, :]
                    real = real + (cosine * child_real - sine * child_imag)
                    imag = imag + (cosine * child_imag + sine * child_real)
                merged = jnp.concatenate([real, imag], axis=0).astype(jnp.bfloat16)
                if level < levels - 1:
                    keep(level + 1, owner, block, merged)
                else:
                    send[owner * beams + block] = merged

    for step in range(1, count):
        copy = pltpu.make_async_remote_copy(
            src_ref=send.at[ahead(step)], dst_ref=landed.at[me],
            send_sem=out_send.at[step], recv_sem=out_recv.at[me],
            device_id=place(ahead(step)), device_id_type=MESH,
        )
        copy.start()
        out_copies.append(copy)
    landed[me] = send[me]
    for step in range(1, count):
        source = ahead(count - step)
        pltpu.make_async_remote_copy(
            src_ref=send.at[source], dst_ref=landed.at[source],
            send_sem=out_send.at[step], recv_sem=out_recv.at[source],
            device_id=place(source), device_id_type=MESH,
        ).wait_recv()
    for part in range(2):
        strips = [landed[source].astype(jnp.float32) for source in range(count)]
        whole = [strip[part * ranges : (part + 1) * ranges] for strip in strips]
        out_ref[part] = jnp.concatenate(whole, axis=0).T.astype(jnp.bfloat16)
    for step in range(1, count):
        out_copies[step - 1].wait_send()
    for step in range(1, half_count):
        own_copies[step].wait_send()
        far_copies[step].wait_send()
        near_copies[step].wait_send()
    for owner in range(subs):
        sum_copies[owner].wait_send()
    across.wait_send()
    beside.wait_send()
    passed_on.wait_send()


def local_sliced(pulses, owners, interp, pattern, *, subs, beams):
    pulse_count, _, range_len = pulses.shape
    levels, _, _, taps, tile, _ = interp.shape
    count = subs * beams
    ranges = range_len // count
    rows = 2 * ranges
    width = beams * tile
    x = pulses
    angle = two_pi / width * (np.arange(pulse_count)[:, None] * np.arange(width)[None, :] % width)
    steer = np.concatenate([np.cos(angle), np.sin(angle)], axis=1).astype(jnp.bfloat16)
    beam_ids = np.arange(width)[None, :] + 1
    range_ids = np.arange(range_len)[:, None] + 1
    phase = two_pi / phase_modulus * (beam_ids * range_ids % phase_modulus)
    phase = np.stack([np.cos(phase), np.sin(phase)], axis=0).astype(np.float32)
    phase = phase.reshape(2, count, ranges, width).transpose(1, 0, 2, 3)
    scale = 1.0 / math.sqrt(pulse_count * beams)
    vmem = pl.BlockSpec(memory_space=pltpu.VMEM)
    hbm = pl.BlockSpec(memory_space=pltpu.HBM)
    out = pl.pallas_call(
        functools.partial(kernel, (subs, beams, ranges, tile, levels, scale)),
        out_shape=jax.ShapeDtypeStruct((2, tile, range_len), jnp.bfloat16),
        in_specs=[hbm, hbm, hbm, pl.BlockSpec(memory_space=pltpu.SMEM), hbm, hbm],
        out_specs=vmem,
        scratch_shapes=[
            pltpu.VMEM(x.shape, jnp.float32),
            pltpu.VMEM((2, range_len, pulse_count), jnp.float32),
            pltpu.VMEM((count, rows, pulse_count), jnp.bfloat16),
            pltpu.VMEM(steer.shape, jnp.bfloat16),
            pltpu.VMEM(phase.shape[1:], jnp.float32),
            pltpu.VMEM((count, rows, pulse_count), jnp.bfloat16),
            pltpu.VMEM((count, 1, pulse_count), jnp.int32),
            pltpu.VMEM((4,) + interp.shape, jnp.bfloat16),
            pltpu.VMEM((subs, rows, pulse_count), jnp.float32),
            pltpu.VMEM((subs, rows, pulse_count), jnp.float32),
            pltpu.VMEM((subs, rows, pulse_count), jnp.bfloat16),
            pltpu.VMEM((subs, rows, pulse_count), jnp.bfloat16),
            pltpu.VMEM((subs * rows, pulse_count), jnp.bfloat16),
            pltpu.VMEM((4 * levels, 2, ranges, width), jnp.float32),
            pltpu.VMEM((beams, 2, subs // 2 * rows, tile), jnp.bfloat16),
            pltpu.VMEM((beams, 2, subs // 2 * rows, tile), jnp.float32),
            pltpu.VMEM((count, rows, tile), jnp.bfloat16),
            pltpu.VMEM((count, rows, tile), jnp.bfloat16),
        ]
        + [pltpu.SemaphoreType.DMA((5,))]
        + [pltpu.SemaphoreType.DMA((count,))] * 4
        + [pltpu.SemaphoreType.DMA((4,))] * 2
        + [pltpu.SemaphoreType.DMA((count,))] * 2
        + [pltpu.SemaphoreType.DMA((subs,))] * 2,
        compiler_params=pltpu.CompilerParams(
            collective_id=0, has_side_effects=True, vmem_limit_bytes=62 * 2**20
        ),
    )(x, owners.reshape(1, pulse_count), interp, pattern.transpose(0, 2, 1), steer, phase)
    return out.transpose(1, 0, 2)[None]


def solution(mesh):
    subs, beams = mesh.shape["sub"], mesh.shape["beam"]

    def local(pulses, owners, interp, pattern):
        pulse_count, _, range_len = pulses.shape
        levels, _, tiles_here, taps, tile, _ = interp.shape
        if (
            range_len % (8 * subs * beams) == 0
            and range_len % 128 == 0
            and beams == 4
            and subs == 1 << levels
            and tiles_here == 1
            and taps == 2
            and pulse_count % (beams * tile) == 0
            and tile % 128 == 0
        ):
            return local_sliced(pulses, owners, interp, pattern, subs=subs, beams=beams)
        return local_general(pulses, owners, interp, pattern)

    in_specs = (
        P(("groups", "sub", "beam"), None, None),
        P(("groups", "sub", "beam"), None),
        P(None, None, "beam", None, None, None),
        P(),
    )
    out_specs = P(("groups", "sub"), "beam", None, None)
    return jax.shard_map(local, mesh=mesh, in_specs=in_specs, out_specs=out_specs, check_vma=False)
```

```python
import functools
import math

import jax
import jax.numpy as jnp
import numpy as np
from jax import lax
from jax.experimental import pallas as pl
from jax.experimental.pallas import tpu as pltpu
from jax.sharding import PartitionSpec as P

two_pi = 2.0 * math.pi
phase_modulus = 1021


def partner_2(block, axis, bit):
    count = lax.axis_size(axis)
    route = []
    for low in range(count):
        high = low | 1 << bit
        if high != low and high < count:
            route += [(low, high), (high, low)]
    return lax.ppermute(block, axis, route)


def steer_terms(beam_rows, sample_positions, beam_count):
    turns = beam_rows[:, None] * sample_positions[None, :] % beam_count
    angle = turns.astype(jnp.float32) * (two_pi / beam_count)
    return (jnp.cos(angle), jnp.sin(angle))


def beamform(cosine, sine, samples):
    range_len = samples.shape[2]
    flat = samples.reshape(samples.shape[0], 2 * range_len)
    first = jnp.dot(
        cosine, flat, precision=lax.Precision.HIGHEST, preferred_element_type=jnp.float32
    )
    second = jnp.dot(
        sine, flat, precision=lax.Precision.HIGHEST, preferred_element_type=jnp.float32
    )
    first = first.reshape(-1, 2, range_len)
    second = second.reshape(-1, 2, range_len)
    real_part = first[:, 0] + second[:, 1]
    imag_part = first[:, 1] - second[:, 0]
    return jnp.stack([real_part, imag_part], axis=1)


def phase_table(level, half, role, beam_rows, range_len):
    beam_ids = beam_rows[:, None] + 1
    range_ids = jnp.arange(range_len, dtype=jnp.int32)[None, :] + 1
    factor = 4 * level + 2 * half + role + 1
    turns = beam_ids * range_ids * factor % phase_modulus
    angle = turns.astype(jnp.float32) * (two_pi / phase_modulus)
    return (jnp.cos(angle), jnp.sin(angle))


def rotate(term, cosine, sine):
    real_part = cosine * term[:, 0] - sine * term[:, 1]
    imag_part = cosine * term[:, 1] + sine * term[:, 0]
    return jnp.stack([real_part, imag_part], axis=1)


def local_general(pulses, owners, interp, pattern):
    sub_count = lax.axis_size("sub")
    beam_count = lax.axis_size("beam")
    sub_index = lax.axis_index("sub")
    beam_index = lax.axis_index("beam")
    pulse_count = pulses.shape[0]
    range_len = pulses.shape[2]
    levels = interp.shape[0]
    tiles_here = interp.shape[2]
    tile_row_block = interp.shape[-1]
    beam_here = tiles_here * tile_row_block
    beam_total = beam_here * beam_count
    capacity = max(2, 2 * pulse_count // sub_count)
    slot_total = sub_count * capacity
    owner_list = owners[:, 0]
    member = (owner_list[:, None] == jnp.arange(sub_count, dtype=jnp.int32)[None, :]).astype(
        jnp.int32
    )
    earlier = jnp.cumsum(member, axis=0) - member
    slot_rank = jnp.sum(earlier * member, axis=1)
    target = owner_list * capacity + slot_rank
    placing = (target[None, :] == jnp.arange(slot_total, dtype=jnp.int32)[:, None]).astype(
        jnp.float32
    )
    device_rank = sub_index * beam_count + beam_index
    sample_positions = (
        device_rank * pulse_count + jnp.arange(pulse_count, dtype=jnp.int32)
    ).astype(jnp.float32)
    send_samples = jnp.dot(
        placing,
        pulses.reshape(pulse_count, 2 * range_len),
        precision=lax.Precision.HIGHEST,
        preferred_element_type=jnp.float32,
    )
    send_samples = send_samples.reshape(sub_count, capacity, 2, range_len)
    send_positions = jnp.dot(
        placing,
        sample_positions,
        precision=lax.Precision.HIGHEST,
        preferred_element_type=jnp.float32,
    )
    send_positions = send_positions.reshape(sub_count, capacity)
    got_samples, got_positions = (
        lax.all_to_all(send_samples, "sub", split_axis=0, concat_axis=0, tiled=True),
        lax.all_to_all(send_positions, "sub", split_axis=0, concat_axis=0, tiled=True),
    )
    got_samples = got_samples.reshape(slot_total, 2, range_len)
    got_positions = got_positions.reshape(slot_total)
    scale = 1.0 / math.sqrt(pulse_count * beam_count)
    my_rows = beam_index * beam_here + jnp.arange(beam_here, dtype=jnp.int32)
    slot_positions = got_positions.astype(jnp.int32)
    rows = jnp.arange(beam_here * lax.axis_size("beam"), dtype=jnp.int32)
    partial_cosine, partial_sine = steer_terms(rows, slot_positions, beam_total)
    base = lax.psum_scatter(
        beamform(partial_cosine, partial_sine, got_samples), "beam", scatter_dimension=0, tiled=True
    )
    image = (scale * base).astype(jnp.bfloat16)
    for level in range(levels):
        half = sub_index >> level & 1
        local_access_pattern = lax.dynamic_slice_in_dim(
            pattern[level], beam_index * tiles_here, tiles_here, 0
        )
        own_weights = lax.dynamic_index_in_dim(interp[level], half, 0, keepdims=False)
        other_weights = lax.dynamic_index_in_dim(interp[level], 1 - half, 0, keepdims=False)

        def taps_sum(interp_weight_table, piece):
            piece_tiles = piece.reshape(-1, tile_row_block, 2 * range_len)
            tile_count = piece_tiles.shape[0]
            inside = (local_access_pattern >= 0) & (local_access_pattern < tile_count)
            selected_entries = piece_tiles[jnp.clip(local_access_pattern, 0, tile_count - 1)]
            selected_entries = jnp.where(
                inside[:, :, None, None], selected_entries, jnp.zeros((), jnp.bfloat16)
            )
            return jnp.einsum(
                "jvlx,jvxu->jlu",
                interp_weight_table,
                selected_entries,
                preferred_element_type=jnp.float32,
            )

        partner = partner_2(image, "sub", level)
        local_term_value = taps_sum(own_weights, lax.all_gather(image, "beam", axis=0, tiled=True))
        other_term = taps_sum(other_weights, lax.all_gather(partner, "beam", axis=0, tiled=True))
        merged = jnp.zeros((beam_here, 2, range_len), jnp.float32)
        for term_part, role in ((local_term_value, half), (other_term, 1 - half)):
            term = term_part.reshape(beam_here, 2, range_len)
            cosine, sine = phase_table(level, half, role, my_rows, range_len)
            merged = merged + rotate(term, cosine, sine)
        image = merged.astype(jnp.bfloat16)
    return image[None]


MESH = pl.DeviceIdType.MESH


def kernel(
    dims, raw_ref, own_ref, interp_ref, pattern_ref, steer_ref, phase_ref, out_ref,
    raw, spread, pieces, steer, phase, got, got_own, weights, sums, far_sums, far_out, far_in, summed, turns, image, term, send, landed,
    local_sem, pulse_send, pulse_recv, own_send, own_recv, weight_send, weight_recv, out_send, out_recv, sum_send, sum_recv,
):
    subs, beams, ranges, tile, levels, scale = dims
    count = subs * beams
    rows = 2 * ranges
    group = lax.axis_index("groups")
    beam = lax.axis_index("beam")
    me = lax.axis_index("sub") * beams + beam

    def place(peer):
        return (group, peer // beams, peer % beams)

    def ahead(step):
        return lax.rem(me + step, count)

    barrier = pltpu.get_barrier_semaphore()
    for step in range(1, count):
        pl.semaphore_signal(barrier, inc=1, device_id=place(ahead(step)), device_id_type=MESH)

    staged = [
        pltpu.make_async_copy(source, target, local_sem.at[number])
        for number, (source, target) in enumerate(
            [
                (raw_ref, raw),
                (interp_ref, weights.at[0]),
                (own_ref, got_own.at[0]),
                (phase_ref.at[me], phase),
                (steer_ref, steer),
            ]
        )
    ]
    for copy in staged:
        copy.start()

    span = spread.shape[1]
    lane_tiles = span // 128
    pulse_count = spread.shape[2]
    staged[0].wait()
    for lane_tile in range(lane_tiles):
        for part in range(2):
            block = raw[:, part, pl.ds(128 * lane_tile, 128)]
            spread[part, pl.ds(128 * lane_tile, 128), :] = block.T
    for piece in range(count):
        at = pl.ds(piece * ranges, ranges)
        both = jnp.concatenate([spread[0, at, :], spread[1, at, :]], axis=0)
        pieces[piece] = both.astype(jnp.bfloat16)
    for copy in staged[1:]:
        copy.wait()
    pl.semaphore_wait(barrier, count - 1)

    half_count = count // 2
    base_peer = me // half_count * half_count
    far = ahead(half_count)
    far_base = half_count - base_peer

    def beside_me(step):
        return lax.rem(me - base_peer + step, half_count)

    def pulse_copy(piece, slot, peer):
        return pltpu.make_async_remote_copy(
            src_ref=pieces.at[piece], dst_ref=got.at[slot],
            send_sem=pulse_send.at[slot], recv_sem=pulse_recv.at[slot],
            device_id=place(peer), device_id_type=MESH,
        )

    own_copies, far_copies, near_copies = [None], [None], [None]
    for step in range(1, half_count):
        peer = base_peer + beside_me(step)
        own_copy = pltpu.make_async_remote_copy(
            src_ref=got_own.at[0], dst_ref=got_own.at[step],
            send_sem=own_send.at[step], recv_sem=own_recv.at[step],
            device_id=place(peer), device_id_type=MESH,
        )
        own_copy.start()
        own_copies.append(own_copy)
        far_copies.append(pulse_copy(far_base + beside_me(step), step, peer))
        far_copies[step].start()
    for step in range(1, half_count):
        peer = base_peer + beside_me(step)
        near_copies.append(pulse_copy(peer, half_count + step, peer))
        near_copies[step].start()

    def beam_at(slot):
        return lax.rem(beam // 2 + slot // 2, 2) * 2 + lax.rem(beam % 2 + slot % 2, 2)

    def weight_copy(source, slot, toward):
        return pltpu.make_async_remote_copy(
            src_ref=source, dst_ref=weights.at[slot],
            send_sem=weight_send.at[slot], recv_sem=weight_recv.at[slot],
            device_id=(group, lax.axis_index("sub"), beam_at(toward)), device_id_type=MESH,
        )

    across = weight_copy(weights.at[0], 2, 2)
    across.start()
    beside = weight_copy(weights.at[0], 1, 1)
    beside.start()

    first_cos = phase[0]
    first_sin = phase[1]
    power_cos, power_sin = first_cos, first_sin
    for power in range(4 * levels):
        if power:
            power_cos, power_sin = (
                power_cos * first_cos - power_sin * first_sin,
                power_cos * first_sin + power_sin * first_cos,
            )
        turns[power, 0] = power_cos
        turns[power, 1] = power_sin

    def add_in(total, values, owner_row, begin):
        wide = values.astype(jnp.float32)
        for owner in range(subs):
            part = jnp.where(owner_row == owner, wide, 0.0)
            total[owner] = part if begin else total[owner] + part

    add_in(far_sums, pieces[far], got_own[0], True)
    for step in range(1, half_count):
        own_copies[step].wait_recv()
        far_copies[step].wait_recv()
        add_in(far_sums, got[step], got_own[step], False)
    sum_copies = []
    for owner in range(subs):
        far_out[owner] = far_sums[owner].astype(jnp.bfloat16)
        sum_copy = pltpu.make_async_remote_copy(
            src_ref=far_out.at[owner], dst_ref=far_in.at[owner],
            send_sem=sum_send.at[owner], recv_sem=sum_recv.at[owner],
            device_id=place(far), device_id_type=MESH,
        )
        sum_copy.start()
        sum_copies.append(sum_copy)
    add_in(sums, pieces[me], got_own[0], True)

    across.wait_recv()
    passed_on = weight_copy(weights.at[2], 3, 1)
    passed_on.start()

    for step in range(1, half_count):
        near_copies[step].wait_recv()
        add_in(sums, got[half_count + step], got_own[step], False)
    for owner in range(subs):
        sum_copies[owner].wait_recv()
        summed[pl.ds(owner * rows, rows), :] = (
            sums[owner] + far_in[owner].astype(jnp.float32)
        ).astype(jnp.bfloat16)

    turned = jnp.dot(summed[...], steer[...], preferred_element_type=jnp.float32)
    width = turned.shape[1] // 2
    tiles = width // tile

    def members(level, half):
        return [s for s in range(subs) if s >> level & 1 == half]

    def keep(level, owner, block, value):
        half = owner >> level & 1
        at = members(level, half).index(owner) * rows
        image[block, half, at : at + rows, :] = value

    for owner in range(subs):
        part = turned[owner * rows : (owner + 1) * rows]
        real = part[:ranges, :width] + part[ranges:, width:]
        imag = part[ranges:, :width] - part[:ranges, width:]
        base = (scale * jnp.concatenate([real, imag], axis=0)).astype(jnp.bfloat16)
        for block in range(tiles):
            keep(0, owner, block, base[:, block * tile : (block + 1) * tile])

    beside.wait_recv()
    passed_on.wait_recv()

    out_copies = []
    for level in range(levels):
        bit = 1 << level
        for slot in range(tiles):
            block = beam_at(slot)
            for half in range(2):
                value = None
                for tap in range(2):
                    kernel_here = weights[slot, level, half, 0, tap]
                    child = image[pattern_ref[level, tap, block], half]
                    product = lax.dot_general(
                        child, kernel_here, (((1,), (1,)), ((), ())),
                        preferred_element_type=jnp.float32,
                    )
                    value = product if value is None else value + product
                term[block, half] = value
        for owner in range(subs):
            half = owner >> level & 1
            for block in range(tiles):
                real = imag = 0.0
                for role in range(2):
                    child = owner - half * bit + role * bit
                    at = members(level, role).index(child) * rows
                    power = 4 * level + 2 * half + role
                    lanes = pl.ds(block * tile, tile)
                    cosine = turns[power, 0, :, lanes]
                    sine = turns[power, 1, :, lanes]
                    child_real = term[block, role, at : at + ranges, :]
                    child_imag = term[block, role, at + ranges : at + rows, :]
                    real = real + (cosine * child_real - sine * child_imag)
                    imag = imag + (cosine * child_imag + sine * child_real)
                merged = jnp.concatenate([real, imag], axis=0).astype(jnp.bfloat16)
                if level < levels - 1:
                    keep(level + 1, owner, block, merged)
                else:
                    send[owner * beams + block] = merged

    for step in range(1, count):
        copy = pltpu.make_async_remote_copy(
            src_ref=send.at[ahead(step)], dst_ref=landed.at[me],
            send_sem=out_send.at[step], recv_sem=out_recv.at[me],
            device_id=place(ahead(step)), device_id_type=MESH,
        )
        copy.start()
        out_copies.append(copy)
    landed[me] = send[me]
    for step in range(1, count):
        source = ahead(count - step)
        pltpu.make_async_remote_copy(
            src_ref=send.at[source], dst_ref=landed.at[source],
            send_sem=out_send.at[step], recv_sem=out_recv.at[source],
            device_id=place(source), device_id_type=MESH,
        ).wait_recv()
    for part in range(2):
        strips = [landed[source].astype(jnp.float32) for source in range(count)]
        whole = [strip[part * ranges : (part + 1) * ranges] for strip in strips]
        out_ref[part] = jnp.concatenate(whole, axis=0).T.astype(jnp.bfloat16)
    for step in range(1, count):
        out_copies[step - 1].wait_send()
    for step in range(1, half_count):
        own_copies[step].wait_send()
        far_copies[step].wait_send()
        near_copies[step].wait_send()
    for owner in range(subs):
        sum_copies[owner].wait_send()
    across.wait_send()
    beside.wait_send()
    passed_on.wait_send()


def local_sliced(pulses, owners, interp, pattern, *, subs, beams):
    pulse_count, _, range_len = pulses.shape
    levels, _, _, taps, tile, _ = interp.shape
    count = subs * beams
    ranges = range_len // count
    rows = 2 * ranges
    width = beams * tile
    x = pulses
    angle = two_pi / width * (np.arange(pulse_count)[:, None] * np.arange(width)[None, :] % width)
    steer = np.concatenate([np.cos(angle), np.sin(angle)], axis=1).astype(jnp.bfloat16)
    beam_ids = np.arange(width)[None, :] + 1
    range_ids = np.arange(range_len)[:, None] + 1
    phase = two_pi / phase_modulus * (beam_ids * range_ids % phase_modulus)
    phase = np.stack([np.cos(phase), np.sin(phase)], axis=0).astype(np.float32)
    phase = phase.reshape(2, count, ranges, width).transpose(1, 0, 2, 3)
    scale = 1.0 / math.sqrt(pulse_count * beams)
    vmem = pl.BlockSpec(memory_space=pltpu.VMEM)
    hbm = pl.BlockSpec(memory_space=pltpu.HBM)
    out = pl.pallas_call(
        functools.partial(kernel, (subs, beams, ranges, tile, levels, scale)),
        out_shape=jax.ShapeDtypeStruct((2, tile, range_len), jnp.bfloat16),
        in_specs=[hbm, hbm, hbm, pl.BlockSpec(memory_space=pltpu.SMEM), hbm, hbm],
        out_specs=vmem,
        scratch_shapes=[
            pltpu.VMEM(x.shape, jnp.float32),
            pltpu.VMEM((2, range_len, pulse_count), jnp.float32),
            pltpu.VMEM((count, rows, pulse_count), jnp.bfloat16),
            pltpu.VMEM(steer.shape, jnp.bfloat16),
            pltpu.VMEM(phase.shape[1:], jnp.float32),
            pltpu.VMEM((count, rows, pulse_count), jnp.bfloat16),
            pltpu.VMEM((count, 1, pulse_count), jnp.int32),
            pltpu.VMEM((4,) + interp.shape, jnp.bfloat16),
            pltpu.VMEM((subs, rows, pulse_count), jnp.float32),
            pltpu.VMEM((subs, rows, pulse_count), jnp.float32),
            pltpu.VMEM((subs, rows, pulse_count), jnp.bfloat16),
            pltpu.VMEM((subs, rows, pulse_count), jnp.bfloat16),
            pltpu.VMEM((subs * rows, pulse_count), jnp.bfloat16),
            pltpu.VMEM((4 * levels, 2, ranges, width), jnp.float32),
            pltpu.VMEM((beams, 2, subs // 2 * rows, tile), jnp.bfloat16),
            pltpu.VMEM((beams, 2, subs // 2 * rows, tile), jnp.float32),
            pltpu.VMEM((count, rows, tile), jnp.bfloat16),
            pltpu.VMEM((count, rows, tile), jnp.bfloat16),
        ]
        + [pltpu.SemaphoreType.DMA((5,))]
        + [pltpu.SemaphoreType.DMA((count,))] * 4
        + [pltpu.SemaphoreType.DMA((4,))] * 2
        + [pltpu.SemaphoreType.DMA((count,))] * 2
        + [pltpu.SemaphoreType.DMA((subs,))] * 2,
        compiler_params=pltpu.CompilerParams(
            collective_id=0, has_side_effects=True, vmem_limit_bytes=107 * 2**19
        ),
    )(x, owners.reshape(1, pulse_count), interp, pattern.transpose(0, 2, 1), steer, phase)
    return out.transpose(1, 0, 2)[None]


def solution(mesh):
    subs, beams = mesh.shape["sub"], mesh.shape["beam"]

    def local(pulses, owners, interp, pattern):
        pulse_count, _, range_len = pulses.shape
        levels, _, tiles_here, taps, tile, _ = interp.shape
        if (
            range_len % (8 * subs * beams) == 0
            and range_len % 128 == 0
            and beams == 4
            and subs == 1 << levels
            and tiles_here == 1
            and taps == 2
            and pulse_count % (beams * tile) == 0
            and tile % 128 == 0
        ):
            return local_sliced(pulses, owners, interp, pattern, subs=subs, beams=beams)
        return local_general(pulses, owners, interp, pattern)

    in_specs = (
        P(("groups", "sub", "beam"), None, None),
        P(("groups", "sub", "beam"), None),
        P(None, None, "beam", None, None, None),
        P(),
    )
    out_specs = P(("groups", "sub"), "beam", None, None)
    return jax.shard_map(local, mesh=mesh, in_specs=in_specs, out_specs=out_specs, check_vma=False)
```

```python
import functools
import math

import jax
import jax.numpy as jnp
import numpy as np
from jax import lax
from jax.experimental import pallas as pl
from jax.experimental.pallas import tpu as pltpu
from jax.sharding import PartitionSpec as P

two_pi = 2.0 * math.pi
phase_modulus = 1021


def partner_2(block, axis, bit):
    count = lax.axis_size(axis)
    route = []
    for low in range(count):
        high = low | 1 << bit
        if high != low and high < count:
            route += [(low, high), (high, low)]
    return lax.ppermute(block, axis, route)


def steer_terms(beam_rows, sample_positions, beam_count):
    turns = beam_rows[:, None] * sample_positions[None, :] % beam_count
    angle = turns.astype(jnp.float32) * (two_pi / beam_count)
    return (jnp.cos(angle), jnp.sin(angle))


def beamform(cosine, sine, samples):
    range_len = samples.shape[2]
    flat = samples.reshape(samples.shape[0], 2 * range_len)
    first = jnp.dot(
        cosine, flat, precision=lax.Precision.HIGHEST, preferred_element_type=jnp.float32
    )
    second = jnp.dot(
        sine, flat, precision=lax.Precision.HIGHEST, preferred_element_type=jnp.float32
    )
    first = first.reshape(-1, 2, range_len)
    second = second.reshape(-1, 2, range_len)
    real_part = first[:, 0] + second[:, 1]
    imag_part = first[:, 1] - second[:, 0]
    return jnp.stack([real_part, imag_part], axis=1)


def phase_table(level, half, role, beam_rows, range_len):
    beam_ids = beam_rows[:, None] + 1
    range_ids = jnp.arange(range_len, dtype=jnp.int32)[None, :] + 1
    factor = 4 * level + 2 * half + role + 1
    turns = beam_ids * range_ids * factor % phase_modulus
    angle = turns.astype(jnp.float32) * (two_pi / phase_modulus)
    return (jnp.cos(angle), jnp.sin(angle))


def rotate(term, cosine, sine):
    real_part = cosine * term[:, 0] - sine * term[:, 1]
    imag_part = cosine * term[:, 1] + sine * term[:, 0]
    return jnp.stack([real_part, imag_part], axis=1)


def local_general(pulses, owners, interp, pattern):
    sub_count = lax.axis_size("sub")
    beam_count = lax.axis_size("beam")
    sub_index = lax.axis_index("sub")
    beam_index = lax.axis_index("beam")
    pulse_count = pulses.shape[0]
    range_len = pulses.shape[2]
    levels = interp.shape[0]
    tiles_here = interp.shape[2]
    tile_row_block = interp.shape[-1]
    beam_here = tiles_here * tile_row_block
    beam_total = beam_here * beam_count
    capacity = max(2, 2 * pulse_count // sub_count)
    slot_total = sub_count * capacity
    owner_list = owners[:, 0]
    member = (owner_list[:, None] == jnp.arange(sub_count, dtype=jnp.int32)[None, :]).astype(
        jnp.int32
    )
    earlier = jnp.cumsum(member, axis=0) - member
    slot_rank = jnp.sum(earlier * member, axis=1)
    target = owner_list * capacity + slot_rank
    placing = (target[None, :] == jnp.arange(slot_total, dtype=jnp.int32)[:, None]).astype(
        jnp.float32
    )
    device_rank = sub_index * beam_count + beam_index
    sample_positions = (
        device_rank * pulse_count + jnp.arange(pulse_count, dtype=jnp.int32)
    ).astype(jnp.float32)
    send_samples = jnp.dot(
        placing,
        pulses.reshape(pulse_count, 2 * range_len),
        precision=lax.Precision.HIGHEST,
        preferred_element_type=jnp.float32,
    )
    send_samples = send_samples.reshape(sub_count, capacity, 2, range_len)
    send_positions = jnp.dot(
        placing,
        sample_positions,
        precision=lax.Precision.HIGHEST,
        preferred_element_type=jnp.float32,
    )
    send_positions = send_positions.reshape(sub_count, capacity)
    got_samples, got_positions = (
        lax.all_to_all(send_samples, "sub", split_axis=0, concat_axis=0, tiled=True),
        lax.all_to_all(send_positions, "sub", split_axis=0, concat_axis=0, tiled=True),
    )
    got_samples = got_samples.reshape(slot_total, 2, range_len)
    got_positions = got_positions.reshape(slot_total)
    scale = 1.0 / math.sqrt(pulse_count * beam_count)
    my_rows = beam_index * beam_here + jnp.arange(beam_here, dtype=jnp.int32)
    slot_positions = got_positions.astype(jnp.int32)
    rows = jnp.arange(beam_here * lax.axis_size("beam"), dtype=jnp.int32)
    partial_cosine, partial_sine = steer_terms(rows, slot_positions, beam_total)
    base = lax.psum_scatter(
        beamform(partial_cosine, partial_sine, got_samples), "beam", scatter_dimension=0, tiled=True
    )
    image = (scale * base).astype(jnp.bfloat16)
    for level in range(levels):
        half = sub_index >> level & 1
        local_access_pattern = lax.dynamic_slice_in_dim(
            pattern[level], beam_index * tiles_here, tiles_here, 0
        )
        own_weights = lax.dynamic_index_in_dim(interp[level], half, 0, keepdims=False)
        other_weights = lax.dynamic_index_in_dim(interp[level], 1 - half, 0, keepdims=False)

        def taps_sum(interp_weight_table, piece):
            piece_tiles = piece.reshape(-1, tile_row_block, 2 * range_len)
            tile_count = piece_tiles.shape[0]
            inside = (local_access_pattern >= 0) & (local_access_pattern < tile_count)
            selected_entries = piece_tiles[jnp.clip(local_access_pattern, 0, tile_count - 1)]
            selected_entries = jnp.where(
                inside[:, :, None, None], selected_entries, jnp.zeros((), jnp.bfloat16)
            )
            return jnp.einsum(
                "jvlx,jvxu->jlu",
                interp_weight_table,
                selected_entries,
                preferred_element_type=jnp.float32,
            )

        partner = partner_2(image, "sub", level)
        local_term_value = taps_sum(own_weights, lax.all_gather(image, "beam", axis=0, tiled=True))
        other_term = taps_sum(other_weights, lax.all_gather(partner, "beam", axis=0, tiled=True))
        merged = jnp.zeros((beam_here, 2, range_len), jnp.float32)
        for term_part, role in ((local_term_value, half), (other_term, 1 - half)):
            term = term_part.reshape(beam_here, 2, range_len)
            cosine, sine = phase_table(level, half, role, my_rows, range_len)
            merged = merged + rotate(term, cosine, sine)
        image = merged.astype(jnp.bfloat16)
    return image[None]


MESH = pl.DeviceIdType.MESH


def kernel(
    dims, raw_ref, own_ref, interp_ref, pattern_ref, steer_ref, phase_ref, out_ref,
    raw, spread, pieces, steer, phase, got, got_own, weights, sums, far_sums, far_out, far_in, summed, turns, image, term, send, landed,
    local_sem, pulse_send, pulse_recv, own_send, own_recv, weight_send, weight_recv, out_send, out_recv, sum_send, sum_recv,
):
    subs, beams, ranges, tile, levels, scale = dims
    count = subs * beams
    rows = 2 * ranges
    group = lax.axis_index("groups")
    beam = lax.axis_index("beam")
    me = lax.axis_index("sub") * beams + beam

    def place(peer):
        return (group, peer // beams, peer % beams)

    def ahead(step):
        return lax.rem(me + step, count)

    barrier = pltpu.get_barrier_semaphore()
    for step in range(1, count):
        pl.semaphore_signal(barrier, inc=1, device_id=place(ahead(step)), device_id_type=MESH)

    staged = [
        pltpu.make_async_copy(source, target, local_sem.at[number])
        for number, (source, target) in enumerate(
            [
                (raw_ref, raw),
                (interp_ref, weights.at[0]),
                (own_ref, got_own.at[0]),
                (phase_ref.at[me], phase),
                (steer_ref, steer),
            ]
        )
    ]
    for copy in staged:
        copy.start()

    span = spread.shape[1]
    lane_tiles = span // 128
    pulse_count = spread.shape[2]
    staged[0].wait()
    for lane_tile in range(lane_tiles):
        for part in range(2):
            block = raw[:, part, pl.ds(128 * lane_tile, 128)]
            spread[part, pl.ds(128 * lane_tile, 128), :] = block.T
    for piece in range(count):
        at = pl.ds(piece * ranges, ranges)
        both = jnp.concatenate([spread[0, at, :], spread[1, at, :]], axis=0)
        pieces[piece] = both.astype(jnp.bfloat16)
    for copy in staged[1:]:
        copy.wait()
    pl.semaphore_wait(barrier, count - 1)

    half_count = count // 2
    base_peer = me // half_count * half_count
    far = ahead(half_count)
    far_base = half_count - base_peer

    def beside_me(step):
        return lax.rem(me - base_peer + step, half_count)

    def pulse_copy(piece, slot, peer):
        return pltpu.make_async_remote_copy(
            src_ref=pieces.at[piece], dst_ref=got.at[slot],
            send_sem=pulse_send.at[slot], recv_sem=pulse_recv.at[slot],
            device_id=place(peer), device_id_type=MESH,
        )

    own_copies, far_copies, near_copies = [None], [None], [None]
    for step in range(1, half_count):
        peer = base_peer + beside_me(step)
        own_copy = pltpu.make_async_remote_copy(
            src_ref=got_own.at[0], dst_ref=got_own.at[step],
            send_sem=own_send.at[step], recv_sem=own_recv.at[step],
            device_id=place(peer), device_id_type=MESH,
        )
        own_copy.start()
        own_copies.append(own_copy)
        far_copies.append(pulse_copy(far_base + beside_me(step), step, peer))
        far_copies[step].start()
    for step in range(1, half_count):
        peer = base_peer + beside_me(step)
        near_copies.append(pulse_copy(peer, half_count + step, peer))
        near_copies[step].start()

    def beam_at(slot):
        return lax.rem(beam // 2 + slot // 2, 2) * 2 + lax.rem(beam % 2 + slot % 2, 2)

    def weight_copy(source, slot, toward):
        return pltpu.make_async_remote_copy(
            src_ref=source, dst_ref=weights.at[slot],
            send_sem=weight_send.at[slot], recv_sem=weight_recv.at[slot],
            device_id=(group, lax.axis_index("sub"), beam_at(toward)), device_id_type=MESH,
        )

    across = weight_copy(weights.at[0], 2, 2)
    across.start()
    beside = weight_copy(weights.at[0], 1, 1)
    beside.start()

    first_cos = phase[0]
    first_sin = phase[1]
    power_cos, power_sin = first_cos, first_sin
    for power in range(4 * levels):
        if power:
            power_cos, power_sin = (
                power_cos * first_cos - power_sin * first_sin,
                power_cos * first_sin + power_sin * first_cos,
            )
        turns[power, 0] = power_cos
        turns[power, 1] = power_sin

    def add_in(total, values, owner_row, begin):
        wide = values.astype(jnp.float32)
        for owner in range(subs):
            part = jnp.where(owner_row == owner, wide, 0.0)
            total[owner] = part if begin else total[owner] + part

    add_in(far_sums, pieces[far], got_own[0], True)
    for step in range(1, half_count):
        own_copies[step].wait_recv()
        far_copies[step].wait_recv()
        add_in(far_sums, got[step], got_own[step], False)
    sum_copies = []
    for owner in range(subs):
        far_out[owner] = far_sums[owner].astype(jnp.bfloat16)
        sum_copy = pltpu.make_async_remote_copy(
            src_ref=far_out.at[owner], dst_ref=far_in.at[owner],
            send_sem=sum_send.at[owner], recv_sem=sum_recv.at[owner],
            device_id=place(far), device_id_type=MESH,
        )
        sum_copy.start()
        sum_copies.append(sum_copy)
    add_in(sums, pieces[me], got_own[0], True)

    across.wait_recv()
    passed_on = weight_copy(weights.at[2], 3, 1)
    passed_on.start()

    for step in range(1, half_count):
        near_copies[step].wait_recv()
        add_in(sums, got[half_count + step], got_own[step], False)
    for owner in range(subs):
        sum_copies[owner].wait_recv()
        summed[pl.ds(owner * rows, rows), :] = (
            sums[owner] + far_in[owner].astype(jnp.float32)
        ).astype(jnp.bfloat16)

    turned = jnp.dot(summed[...], steer[...], preferred_element_type=jnp.float32)
    width = turned.shape[1] // 2
    tiles = width // tile

    def members(level, half):
        return [s for s in range(subs) if s >> level & 1 == half]

    def keep(level, owner, block, value):
        half = owner >> level & 1
        at = members(level, half).index(owner) * rows
        image[block, half, at : at + rows, :] = value

    for owner in range(subs):
        part = turned[owner * rows : (owner + 1) * rows]
        real = part[:ranges, :width] + part[ranges:, width:]
        imag = part[ranges:, :width] - part[:ranges, width:]
        base = (scale * jnp.concatenate([real, imag], axis=0)).astype(jnp.bfloat16)
        for block in range(tiles):
            keep(0, owner, block, base[:, block * tile : (block + 1) * tile])

    beside.wait_recv()
    passed_on.wait_recv()

    def out_copy(peer):
        return pltpu.make_async_remote_copy(
            src_ref=send.at[peer], dst_ref=landed.at[me],
            send_sem=out_send.at[peer], recv_sem=out_recv.at[me],
            device_id=place(peer), device_id_type=MESH,
        )

    def ready(peer):
        @pl.when(peer != me)
        def _():
            out_copy(peer).start()

    for level in range(levels):
        bit = 1 << level
        for slot in range(tiles):
            block = beam_at(slot)
            for half in range(2):
                value = None
                for tap in range(2):
                    kernel_here = weights[slot, level, half, 0, tap]
                    child = image[pattern_ref[level, tap, block], half]
                    product = lax.dot_general(
                        child, kernel_here, (((1,), (1,)), ((), ())),
                        preferred_element_type=jnp.float32,
                    )
                    value = product if value is None else value + product
                term[block, half] = value
        for owner in range(subs):
            half = owner >> level & 1
            for block in range(tiles):
                real = imag = 0.0
                for role in range(2):
                    child = owner - half * bit + role * bit
                    at = members(level, role).index(child) * rows
                    power = 4 * level + 2 * half + role
                    lanes = pl.ds(block * tile, tile)
                    cosine = turns[power, 0, :, lanes]
                    sine = turns[power, 1, :, lanes]
                    child_real = term[block, role, at : at + ranges, :]
                    child_imag = term[block, role, at + ranges : at + rows, :]
                    real = real + (cosine * child_real - sine * child_imag)
                    imag = imag + (cosine * child_imag + sine * child_real)
                merged = jnp.concatenate([real, imag], axis=0).astype(jnp.bfloat16)
                if level < levels - 1:
                    keep(level + 1, owner, block, merged)
                else:
                    send[owner * beams + block] = merged
                    ready(owner * beams + block)

    landed[me] = send[me]
    for step in range(1, count):
        source = ahead(count - step)
        pltpu.make_async_remote_copy(
            src_ref=send.at[source], dst_ref=landed.at[source],
            send_sem=out_send.at[source], recv_sem=out_recv.at[source],
            device_id=place(source), device_id_type=MESH,
        ).wait_recv()
    for part in range(2):
        strips = [landed[source].astype(jnp.float32) for source in range(count)]
        whole = [strip[part * ranges : (part + 1) * ranges] for strip in strips]
        out_ref[part] = jnp.concatenate(whole, axis=0).T.astype(jnp.bfloat16)
    for step in range(1, count):
        out_copy(ahead(step)).wait_send()
    for step in range(1, half_count):
        own_copies[step].wait_send()
        far_copies[step].wait_send()
        near_copies[step].wait_send()
    for owner in range(subs):
        sum_copies[owner].wait_send()
    across.wait_send()
    beside.wait_send()
    passed_on.wait_send()


def local_sliced(pulses, owners, interp, pattern, *, subs, beams):
    pulse_count, _, range_len = pulses.shape
    levels, _, _, taps, tile, _ = interp.shape
    count = subs * beams
    ranges = range_len // count
    rows = 2 * ranges
    width = beams * tile
    x = pulses
    angle = two_pi / width * (np.arange(pulse_count)[:, None] * np.arange(width)[None, :] % width)
    steer = np.concatenate([np.cos(angle), np.sin(angle)], axis=1).astype(jnp.bfloat16)
    beam_ids = np.arange(width)[None, :] + 1
    range_ids = np.arange(range_len)[:, None] + 1
    phase = two_pi / phase_modulus * (beam_ids * range_ids % phase_modulus)
    phase = np.stack([np.cos(phase), np.sin(phase)], axis=0).astype(np.float32)
    phase = phase.reshape(2, count, ranges, width).transpose(1, 0, 2, 3)
    scale = 1.0 / math.sqrt(pulse_count * beams)
    vmem = pl.BlockSpec(memory_space=pltpu.VMEM)
    hbm = pl.BlockSpec(memory_space=pltpu.HBM)
    out = pl.pallas_call(
        functools.partial(kernel, (subs, beams, ranges, tile, levels, scale)),
        out_shape=jax.ShapeDtypeStruct((2, tile, range_len), jnp.bfloat16),
        in_specs=[hbm, hbm, hbm, pl.BlockSpec(memory_space=pltpu.SMEM), hbm, hbm],
        out_specs=vmem,
        scratch_shapes=[
            pltpu.VMEM(x.shape, jnp.float32),
            pltpu.VMEM((2, range_len, pulse_count), jnp.float32),
            pltpu.VMEM((count, rows, pulse_count), jnp.bfloat16),
            pltpu.VMEM(steer.shape, jnp.bfloat16),
            pltpu.VMEM(phase.shape[1:], jnp.float32),
            pltpu.VMEM((count, rows, pulse_count), jnp.bfloat16),
            pltpu.VMEM((count, 1, pulse_count), jnp.int32),
            pltpu.VMEM((4,) + interp.shape, jnp.bfloat16),
            pltpu.VMEM((subs, rows, pulse_count), jnp.float32),
            pltpu.VMEM((subs, rows, pulse_count), jnp.float32),
            pltpu.VMEM((subs, rows, pulse_count), jnp.bfloat16),
            pltpu.VMEM((subs, rows, pulse_count), jnp.bfloat16),
            pltpu.VMEM((subs * rows, pulse_count), jnp.bfloat16),
            pltpu.VMEM((4 * levels, 2, ranges, width), jnp.float32),
            pltpu.VMEM((beams, 2, subs // 2 * rows, tile), jnp.bfloat16),
            pltpu.VMEM((beams, 2, subs // 2 * rows, tile), jnp.float32),
            pltpu.VMEM((count, rows, tile), jnp.bfloat16),
            pltpu.VMEM((count, rows, tile), jnp.bfloat16),
        ]
        + [pltpu.SemaphoreType.DMA((5,))]
        + [pltpu.SemaphoreType.DMA((count,))] * 4
        + [pltpu.SemaphoreType.DMA((4,))] * 2
        + [pltpu.SemaphoreType.DMA((count,))] * 2
        + [pltpu.SemaphoreType.DMA((subs,))] * 2,
        compiler_params=pltpu.CompilerParams(
            collective_id=0, has_side_effects=True, vmem_limit_bytes=107 * 2**19
        ),
    )(x, owners.reshape(1, pulse_count), interp, pattern.transpose(0, 2, 1), steer, phase)
    return out.transpose(1, 0, 2)[None]


def solution(mesh):
    subs, beams = mesh.shape["sub"], mesh.shape["beam"]

    def local(pulses, owners, interp, pattern):
        pulse_count, _, range_len = pulses.shape
        levels, _, tiles_here, taps, tile, _ = interp.shape
        if (
            range_len % (8 * subs * beams) == 0
            and range_len % 128 == 0
            and beams == 4
            and subs == 1 << levels
            and tiles_here == 1
            and taps == 2
            and pulse_count % (beams * tile) == 0
            and tile % 128 == 0
        ):
            return local_sliced(pulses, owners, interp, pattern, subs=subs, beams=beams)
        return local_general(pulses, owners, interp, pattern)

    in_specs = (
        P(("groups", "sub", "beam"), None, None),
        P(("groups", "sub", "beam"), None),
        P(None, None, "beam", None, None, None),
        P(),
    )
    out_specs = P(("groups", "sub"), "beam", None, None)
    return jax.shard_map(local, mesh=mesh, in_specs=in_specs, out_specs=out_specs, check_vma=False)
```
